128 devices in a mesh: dp: 4 (over y), ctx: 32 (over z, x, core).
Axes of the slice: x: 4, y: 4, z: 4, core: 2. Of those that a mesh axis runs over, the one named last changes fastest.
Arguments:
- se_query: bfloat16 [16384, 4096], P(('dp', 'ctx')), parts along dimension 0, may hold values from -6 to 6
- se_key: bfloat16 [16384, 4096], P(('dp', 'ctx')), parts along dimension 0, may hold values from -6 to 6
- se_value: bfloat16 [16384, 4096], P(('dp', 'ctx')), parts along dimension 0, may hold values from -6 to 6
- feature_taps: float32 [3, 3, 4096], replicated, may hold values from -3 to 3
- inner_taps: float32 [7, 4096], replicated, may hold values from -3 to 3
- li_query: bfloat16 [16384, 4096], P(('dp', 'ctx')), parts along dimension 0, may hold values from -6 to 6
- li_key: bfloat16 [16384, 4096], P(('dp', 'ctx')), parts along dimension 0, may hold values from -6 to 6
- long_filter: bfloat16 [4096, 4096], P('ctx'), may hold values from -1 to 1, as said below
Outputs:
- mixed: bfloat16 [16384, 4096], P(('dp', 'ctx')), parts along dimension 0
The draws below stay inside these ranges and needn't reach their ends.
There are 4 independent parts, one for each index of `dp`. The reference program is written for one: setup_inputs(seed, part) draws one part's arguments, and reference() takes and returns one part's arrays. A program takes and returns all parts, laid end to end along the dimension named above; an argument that names none is the same for every part. Nothing has to cross between parts.
Inputs may be any that keep to these rules, and one draw needn't show every extreme that they name: `long_filter`: a causal filter for each channel, rough from lag to lag.
All inputs are finite; a program needn't handle non-finite values.
Results may differ from the reference program's by a relative error of at most 0.011.
Values may be sent and summed in bfloat16 or wider, within the bound.
A program may use at most 128 MiB of HBM per device.

```python
import jax
import jax.numpy as jnp
from jax import lax

C = 4096
FEAT_TAPS = 3
INNER_TAPS = 7
SEQ = 4096


def draw_long_filter(key, part):
    key = jax.random.fold_in(key, 11)
    span_key, rough_key = jax.random.split(key)
    lower = jnp.log(32.0)
    span = jnp.exp(jax.random.uniform(span_key, (1, C), jnp.float32, lower, jnp.log(4.0 * SEQ)))
    rough = jax.random.truncated_normal(rough_key, -4.0, 4.0, (SEQ, C), jnp.float32)
    places = jnp.arange(SEQ, dtype=jnp.float32)[:, None]
    gain = jnp.sqrt(2.0 / jnp.minimum(span, 1.0 * SEQ))
    return (rough * gain * jnp.exp(-places / span)).astype(jnp.bfloat16)


def shard_levels(stream_key, shape, shards, low, high):
    loudness, own = 1.0, jax.random.fold_in(stream_key, 6)
    for axis_at, blocks in shards:
        draws = jnp.exp(jax.random.uniform(jax.random.fold_in(own, axis_at), (blocks,), jnp.float32, low / len(shards), high / len(shards)))
        loudness = loudness * jnp.repeat(draws, shape[axis_at] // blocks).reshape([-1 if axis == axis_at else 1 for axis in range(len(shape))])
    return loudness


def normal_values(key, dims, scale, reach, cuts=(), held_as=jnp.bfloat16):
    level = shard_levels(key, dims, cuts, -0.22, 0.18) if cuts else 1.0
    drawn = jax.random.normal(key, dims, jnp.float32) * scale * level
    return jnp.minimum(jnp.maximum(drawn, -reach), reach).astype(held_as)


def setup_inputs(seed: int = 0, part: int = 0) -> dict:
    key_list = jax.random.split(jax.random.key(seed), 9)
    own_keys = jax.random.split(jax.random.fold_in(key_list[8], part), 9)
    return {
        "se_query": normal_values(own_keys[0], (SEQ, C), 1.0, 6.0, ((0, 32),)),
        "se_key": normal_values(own_keys[1], (SEQ, C), 1.0, 6.0, ((0, 32),)),
        "se_value": normal_values(own_keys[2], (SEQ, C), 1.0, 6.0, ((0, 32),)),
        "feature_taps": normal_values(key_list[3], (3, FEAT_TAPS, C), 0.6, 3.0, (), jnp.float32),
        "inner_taps": normal_values(key_list[4], (INNER_TAPS, C), 0.4, 3.0, (), jnp.float32),
        "li_query": normal_values(own_keys[5], (SEQ, C), 1.0, 6.0, ((0, 32),)),
        "li_key": normal_values(own_keys[6], (SEQ, C), 1.0, 6.0, ((0, 32),)),
        "long_filter": draw_long_filter(jax.random.fold_in(key_list[8], 71), part),
    }


def causal_filter(rows, taps):
    count = taps.shape[0]
    length = rows.shape[0]
    padded = jnp.concatenate([jnp.zeros((count - 1, rows.shape[1]), jnp.float32), rows], axis=0)
    total = jnp.zeros((length, rows.shape[1]), jnp.float32)
    for lag in range(count):
        total = total + taps[lag] * lax.slice_in_dim(padded, count - 1 - lag, count - 1 - lag + length, axis=0)
    return total


def reference(se_query, se_key, se_value, feature_taps, inner_taps, li_query, li_key, long_filter):
    feat_q = causal_filter(se_query.astype(jnp.float32), feature_taps[0])
    feat_k = causal_filter(se_key.astype(jnp.float32), feature_taps[1])
    feat_v = causal_filter(se_value.astype(jnp.float32), feature_taps[2])
    inner = causal_filter(feat_k * feat_v, inner_taps)
    se_out = feat_q * inner
    signal = (li_key.astype(jnp.float32) * se_out).astype(jnp.bfloat16)
    length = 2 * SEQ
    spectrum = jnp.fft.rfft(signal.astype(jnp.float32), n=length, axis=0) * jnp.fft.rfft(long_filter.astype(jnp.float32), n=length, axis=0)
    long_conv = jnp.fft.irfft(spectrum, n=length, axis=0)[:SEQ]
    return (li_query.astype(jnp.float32) * long_conv).astype(jnp.bfloat16)
```

```python
import functools

import jax
import jax.numpy as jnp
import ml_dtypes
import numpy as np
from jax import lax
from jax.experimental import pallas as pl
from jax.experimental.pallas import tpu as pltpu
from jax.sharding import PartitionSpec as P

MESH = pl.DeviceIdType.MESH
F32, BF16 = jnp.float32, jnp.bfloat16
LANES = 128
HALF = 16


def transform_tables(blocks, block):
    n = 2 * blocks * block
    i, b, m = np.arange(blocks), np.arange(block), np.arange(block)
    first = np.zeros((blocks, 2, blocks))
    last = np.zeros((blocks, blocks, 2))
    ahead = np.zeros((blocks, 2 * block, 2 * block))
    back = np.zeros((blocks, 2 * block, 2 * block))
    first[0, 0] = 1.0
    first[0, 1] = (-1.0) ** i
    last[:, 0, 0] = 1.0
    last[:, 0, 1] = (-1.0) ** i
    h = block // 2
    even = 2 * np.pi * np.outer(2 * blocks * m[:h], b) / n
    odd = 2 * np.pi * np.outer(blocks + 2 * blocks * m[:h], b) / n
    ahead[0, :h, :block] = np.cos(even)
    ahead[0, block : block + h, :block] = -np.sin(even)
    ahead[0, block, :block] = (-1.0) ** b
    ahead[0, h:block, block:] = np.cos(odd)
    ahead[0, block + h :, block:] = -np.sin(odd)
    back[0, :block, :h] = 2 * np.cos(even).T
    back[0, :block, 0] = 1.0
    back[0, :block, block : block + h] = -2 * np.sin(even).T
    back[0, :block, block] = (-1.0) ** b
    back[0, block:, h:block] = 2 * np.cos(odd).T
    back[0, block:, block + h :] = -2 * np.sin(odd).T
    for p in range(1, blocks):
        turn = np.pi * i * p / blocks
        first[p, 0], first[p, 1] = np.cos(turn), -np.sin(turn)
        last[:, p, 0], last[:, p, 1] = np.cos(turn), -np.sin(turn)
        angle = 2 * np.pi * np.outer(p + 2 * blocks * m, b) / n
        c, s = np.cos(angle), np.sin(angle)
        ahead[p] = np.block([[c, s], [-s, c]])
        back[p] = 2 * np.block([[c.T, -s.T], [s.T, c.T]])
    same = np.eye(HALF)
    first = np.kron(first.reshape(2 * blocks, blocks), same)
    last = np.kron(last.reshape(blocks, 2 * blocks), same)
    return [t.astype(ml_dtypes.bfloat16) for t in (first, ahead, back / n, last)]


def kernel(
    n, q_hbm, k_hbm, v_hbm, feature_hbm, inner_hbm, key_hbm, filter_hbm, first_hbm, ahead_hbm, back_hbm, last_hbm,
    out_hbm,
    q, k, v, feature, inner, key, first, ahead, back, last,
    edge_out, edge_in, ext, sig_out, sig_in, filt_in, spec, turned, conv_out,
    local_sem, edge_sem, sig_send, sig_recv, filt_send, filt_recv, conv_send, conv_recv,
):
    me = lax.axis_index("ctx")
    right = lax.rem(me + 1, n)
    rows = q.shape[0]

    def other(s):
        return lax.rem(me + s, n)

    def cols(g):
        return pl.ds(pl.multiple_of(g * LANES, LANES), LANES)

    loads = [
        pltpu.make_async_copy(src, dst, local_sem.at[at])
        for at, (src, dst) in enumerate(
            [
                (k_hbm, k), (v_hbm, v), (q_hbm, q), (feature_hbm, feature), (inner_hbm, inner), (key_hbm, key),
                (first_hbm, first), (ahead_hbm, ahead), (back_hbm, back), (last_hbm, last),
                (filter_hbm.at[:, cols(me)], filt_in.at[me]),
            ]
        )
    ]
    for load in loads:
        load.start()

    barrier = pltpu.get_barrier_semaphore()

    @pl.loop(1, n)
    def _(s):
        pl.semaphore_signal(barrier, inc=1, device_id={"ctx": other(s)}, device_id_type=MESH)

    pl.semaphore_wait(barrier, n - 1)

    def filter_copy(s):
        g = other(s)
        return pltpu.make_async_remote_copy(
            src_ref=filter_hbm.at[:, cols(g)], dst_ref=filt_in.at[me],
            send_sem=filt_send, recv_sem=filt_recv.at[me],
            device_id={"ctx": g}, device_id_type=MESH,
        )

    for load in loads[:4]:
        load.wait()

    row8 = lax.broadcasted_iota(jnp.int32, (8, LANES), 0)

    @pl.loop(0, n)
    def _(g):
        at = cols(g)
        k16 = k[pl.ds(rows - 16, 16), at].astype(F32)
        v16 = v[pl.ds(rows - 16, 16), at].astype(F32)
        q16 = q[pl.ds(rows - 16, 16), at].astype(F32)
        fk = jnp.zeros((8, LANES), F32)
        fv = jnp.zeros((8, LANES), F32)
        for lag in range(3):
            fk = fk + feature[1, pl.ds(lag, 1), at] * k16[8 - lag : 16 - lag]
            fv = fv + feature[2, pl.ds(lag, 1), at] * v16[8 - lag : 16 - lag]
        packed = jnp.where(
            row8 < 2, pltpu.roll(q16[8:], 2, 0),
            jnp.where(row8 < 4, pltpu.roll(k16[8:], 4, 0), pltpu.roll(v16[8:], 6, 0)),
        )
        edge_out[:, at] = jnp.concatenate([fk * fv, packed], axis=0).astype(BF16)

    edge_copy = pltpu.make_async_remote_copy(
        src_ref=edge_out, dst_ref=edge_in, send_sem=edge_sem.at[0], recv_sem=edge_sem.at[1],
        device_id={"ctx": right}, device_id_type=MESH,
    )
    edge_copy.start()

    @pl.loop(1, n)
    def _(s):
        filter_copy(s).start()

    for load in loads[4:6]:
        load.wait()
    edge_copy.wait()

    def signal_block(g):
        at = cols(g)
        edge = jnp.where(me > 0, edge_in[:, at].astype(F32), 0.0)
        packed = edge[8:]
        ext[0, pl.ds(0, 8), :] = pltpu.roll(packed, 6, 0)
        ext[1, pl.ds(0, 8), :] = pltpu.roll(packed, 4, 0)
        ext[2, pl.ds(0, 8), :] = pltpu.roll(packed, 2, 0)
        ext[3, pl.ds(0, 8), :] = edge[:8]
        feats = []
        for stream, ref in enumerate((q, k, v)):
            own = ref[:, at].astype(F32)
            ext[stream, pl.ds(8, rows), :] = own
            total = feature[stream, pl.ds(0, 1), at] * own
            for lag in range(1, 3):
                total = total + feature[stream, pl.ds(lag, 1), at] * ext[stream, pl.ds(8 - lag, rows), :]
            feats.append(total)
        product = feats[1] * feats[2]
        ext[3, pl.ds(8, rows), :] = product
        total = inner[pl.ds(0, 1), at] * product
        for lag in range(1, 7):
            total = total + inner[pl.ds(lag, 1), at] * ext[3, pl.ds(8 - lag, rows), :]
        return (key[:, at].astype(F32) * (feats[0] * total)).astype(BF16)

    def signal_copy(s):
        g = other(s)
        return pltpu.make_async_remote_copy(
            src_ref=sig_out.at[g], dst_ref=sig_in.at[me], send_sem=sig_send, recv_sem=sig_recv.at[me],
            device_id={"ctx": g}, device_id_type=MESH,
        )

    @pl.loop(1, n)
    def _(s):
        sig_out[other(s)] = signal_block(other(s))
        signal_copy(s).start()

    sig_in[me] = signal_block(me)

    def first_step(source, lane):
        @pl.loop(0, rows // 32)
        def _(j):
            at = [pl.ds(pl.multiple_of(j * 32 + 16 * half, 16), 16) for half in range(2)]
            pair = jnp.concatenate([source[:, a, :].reshape(n * 16, LANES) for a in at], axis=1)
            done = jnp.dot(first[...], pair, preferred_element_type=F32).astype(BF16)
            for half in range(2):
                spec[:, at[half], lane : lane + LANES] = done[:, half * LANES : (half + 1) * LANES].reshape(
                    2 * n, 16, LANES
                )

    for load in loads[6:]:
        load.wait()

    def received(landing, sem):
        @pl.loop(1, n)
        def _(s):
            g = other(s)
            pltpu.make_async_copy(landing.at[g], landing.at[g], sem.at[g]).wait()

    received(filt_in, filt_recv)
    first_step(filt_in, LANES)
    received(sig_in, sig_recv)
    first_step(sig_in, 0)

    row = lax.broadcasted_iota(jnp.int32, (rows, LANES), 0)

    @pl.loop(0, n // 4)
    def _(step):
        for u in range(4):
            p = step * 4 + u
            both = jnp.dot(
                ahead[p], spec[pl.ds(2 * p, 2)].reshape(2 * rows, 2 * LANES), preferred_element_type=F32
            )
            xr, hr = both[:rows, :LANES], both[:rows, LANES:]
            xi, hi = both[rows:, :LANES], both[rows:, LANES:]
            real, imag = xr * hr - xi * hi, xr * hi + xi * hr
            if u == 0:
                alone = jnp.logical_and(row == 0, p == 0)
                real = jnp.where(alone, xr * hr, real)
                imag = jnp.where(alone, xi * hi, imag)
            both = jnp.concatenate([real, imag], axis=0).astype(BF16)
            turned[pl.ds(2 * p, 2)] = (
                jnp.dot(back[p], both, preferred_element_type=F32).astype(BF16).reshape(2, rows, LANES)
            )

    def conv_copy(s, part):
        g = other(s)
        at = pl.ds(part * (rows // 2), rows // 2)
        return pltpu.make_async_remote_copy(
            src_ref=conv_out.at[g, at], dst_ref=out_hbm.at[at, cols(me)],
            send_sem=conv_send, recv_sem=conv_recv.at[me],
            device_id={"ctx": g}, device_id_type=MESH,
        )

    for part in range(2):
        @pl.loop(0, rows // 64)
        def _(j):
            at = [pl.ds(pl.multiple_of(part * (rows // 2) + j * 32 + 16 * half, 16), 16) for half in range(2)]
            pair = jnp.concatenate([turned[:, a, :].reshape(2 * n * 16, LANES) for a in at], axis=1)
            done = jnp.dot(last[...], pair, preferred_element_type=F32).astype(BF16)
            for half in range(2):
                conv_out[:, at[half], :] = done[:, half * LANES : (half + 1) * LANES].reshape(n, 16, LANES)

        @pl.loop(1, n)
        def _(s):
            conv_copy(s, part).start()

    own = pltpu.make_async_copy(conv_out.at[me], out_hbm.at[:, cols(me)], local_sem.at[0])
    own.start()
    own.wait()

    @pl.loop(1, n)
    def _(s):
        g = other(s)
        there = out_hbm.at[:, cols(g)]
        pltpu.make_async_copy(there, there, conv_recv.at[g]).wait()

    for ref, sem in ((filt_in, filt_send), (sig_out, sig_send), (conv_out, conv_send)):
        sent = ref.at[pl.ds(0, n - 1)]
        pltpu.make_async_copy(sent, sent, sem).wait()


def solution(mesh):
    n = mesh.shape["ctx"]

    def local(se_query, se_key, se_value, feature_taps, inner_taps, li_query, li_key, long_filter):
        rows, width = se_query.shape
        tables = transform_tables(n, rows)
        block = (n, rows, LANES)
        dma = pltpu.SemaphoreType.DMA
        conv = pl.pallas_call(
            functools.partial(kernel, n),
            out_shape=jax.ShapeDtypeStruct((rows, width), BF16),
            in_specs=[pl.BlockSpec(memory_space=pl.ANY)] * 11,
            out_specs=pl.BlockSpec(memory_space=pl.ANY),
            scratch_shapes=[
                pltpu.VMEM((rows, width), BF16),
                pltpu.VMEM((rows, width), BF16),
                pltpu.VMEM((rows, width), BF16),
                pltpu.VMEM(feature_taps.shape, F32),
                pltpu.VMEM(inner_taps.shape, F32),
                pltpu.VMEM((rows, width), BF16),
                *[pltpu.VMEM(t.shape, BF16) for t in tables],
                pltpu.VMEM((16, width), BF16),
                pltpu.VMEM((16, width), BF16),
                pltpu.VMEM((4, rows + 8, LANES), F32),
                pltpu.VMEM(block, BF16),
                pltpu.VMEM(block, BF16),
                pltpu.VMEM(block, BF16),
                pltpu.VMEM((2 * n, rows, 2 * LANES), BF16),
                pltpu.VMEM((2 * n, rows, LANES), BF16),
                pltpu.VMEM(block, BF16),
                dma((11,)),
                dma((2,)),
                dma,
                dma((n,)),
                dma,
                dma((n,)),
                dma,
                dma((n,)),
            ],
            compiler_params=pltpu.CompilerParams(
                collective_id=0, has_side_effects=True, vmem_limit_bytes=56 * 1024 * 1024
            ),
        )(
            se_query, se_key, se_value, feature_taps, inner_taps, li_key, long_filter,
            *[jnp.asarray(t) for t in tables],
        )
        return (li_query.astype(F32) * conv.astype(F32)).astype(BF16)

    rows_over = P(("dp", "ctx"), None)
    return jax.shard_map(
        local,
        mesh=mesh,
        in_specs=(rows_over, rows_over, rows_over, P(), P(), rows_over, rows_over, P("ctx", None)),
        out_specs=rows_over,
        check_vma=False,
    )
```

```python
import functools

import jax
import jax.numpy as jnp
import ml_dtypes
import numpy as np
from jax import lax
from jax.experimental import pallas as pl
from jax.experimental.pallas import tpu as pltpu
from jax.sharding import PartitionSpec as P

MESH = pl.DeviceIdType.MESH
F32, BF16 = jnp.float32, jnp.bfloat16
LANES = 128
HALF = 16
UNROLL = 16


def transform_tables(blocks, block):
    n = 2 * blocks * block
    i, b, m = np.arange(blocks), np.arange(block), np.arange(block)
    first = np.zeros((blocks, 2, blocks))
    last = np.zeros((blocks, blocks, 2))
    ahead = np.zeros((blocks, 2 * block, 2 * block))
    back = np.zeros((blocks, 2 * block, 2 * block))
    first[0, 0] = 1.0
    first[0, 1] = (-1.0) ** i
    last[:, 0, 0] = 1.0
    last[:, 0, 1] = (-1.0) ** i
    h = block // 2
    even = 2 * np.pi * np.outer(2 * blocks * m[:h], b) / n
    odd = 2 * np.pi * np.outer(blocks + 2 * blocks * m[:h], b) / n
    ahead[0, :h, :block] = np.cos(even)
    ahead[0, block : block + h, :block] = -np.sin(even)
    ahead[0, block, :block] = (-1.0) ** b
    ahead[0, h:block, block:] = np.cos(odd)
    ahead[0, block + h :, block:] = -np.sin(odd)
    back[0, :block, :h] = 2 * np.cos(even).T
    back[0, :block, 0] = 1.0
    back[0, :block, block : block + h] = -2 * np.sin(even).T
    back[0, :block, block] = (-1.0) ** b
    back[0, block:, h:block] = 2 * np.cos(odd).T
    back[0, block:, block + h :] = -2 * np.sin(odd).T
    for p in range(1, blocks):
        turn = np.pi * i * p / blocks
        first[p, 0], first[p, 1] = np.cos(turn), -np.sin(turn)
        last[:, p, 0], last[:, p, 1] = np.cos(turn), -np.sin(turn)
        angle = 2 * np.pi * np.outer(p + 2 * blocks * m, b) / n
        c, s = np.cos(angle), np.sin(angle)
        ahead[p] = np.block([[c, s], [-s, c]])
        back[p] = 2 * np.block([[c.T, -s.T], [s.T, c.T]])
    same = np.eye(HALF)
    first = np.kron(first.reshape(2 * blocks, blocks), same)
    last = np.kron(last.reshape(blocks, 2 * blocks), same)
    return [t.astype(ml_dtypes.bfloat16) for t in (first, ahead, back / n, last)]


def kernel(
    n, groups,
    q_hbm, k_hbm, v_hbm, feature_hbm, inner_hbm, key_hbm, query_hbm, filter_hbm,
    first_hbm, ahead_hbm, back_hbm, last_hbm,
    out_hbm,
    q, k, v, feature, inner, key, query, first, ahead, back, last,
    tails, edge_out, edge_in, ext, sig_out, sig_in, filt_in, sig_spec, filt_spec, filt_freq, product, turned,
    conv_out, conv_in, out,
    local_sem, out_sem, edge_sem, sig_send, sig_recv, filt_send, filt_recv, share_send, share_recv,
    conv_send, conv_recv,
):
    me, part = lax.axis_index("ctx"), lax.axis_index("dp")
    right = lax.rem(me + 1, n)
    above, below = lax.rem(part + 1, groups), lax.rem(part + groups - 1, groups)
    opposite = lax.rem(part + 2, groups)
    rows = q.shape[0]
    mid, quarter = rows // 2, rows // groups

    def other(s):
        return lax.rem(me + s, n)

    def cols(g):
        return pl.ds(pl.multiple_of(g * LANES, LANES), LANES)

    def share(d):
        return pl.ds(pl.multiple_of(d * quarter, quarter), quarter)

    def arrived(ref, sem):
        pltpu.make_async_copy(ref, ref, sem).wait()

    tail = pl.ds(rows - 16, 16)
    loads = [
        pltpu.make_async_copy(src, dst, local_sem.at[at])
        for at, (src, dst) in enumerate(
            [
                (q_hbm.at[tail], tails.at[0]), (k_hbm.at[tail], tails.at[1]), (v_hbm.at[tail], tails.at[2]),
                (feature_hbm, feature),
                (k_hbm, k), (v_hbm, v), (q_hbm, q), (inner_hbm, inner), (key_hbm, key),
                (filter_hbm.at[share(part), cols(me)], filt_in.at[me, share(part)]),
                (first_hbm, first), (ahead_hbm, ahead), (back_hbm, back), (last_hbm, last), (query_hbm, query),
            ]
        )
    ]
    for load in loads[:10]:
        load.start()

    barrier = pltpu.get_barrier_semaphore()

    @pl.loop(1, n)
    def _(s):
        pl.semaphore_signal(barrier, inc=1, device_id={"ctx": other(s)}, device_id_type=MESH)

    for d in (above, below):
        pl.semaphore_signal(barrier, inc=1, device_id={"dp": d}, device_id_type=MESH)

    for load in loads[:4]:
        load.wait()

    row8 = lax.broadcasted_iota(jnp.int32, (8, LANES), 0)

    @pl.loop(0, n)
    def _(g):
        at = cols(g)
        q16, k16, v16 = (tails[stream, :, at].astype(F32) for stream in range(3))
        fk = jnp.zeros((8, LANES), F32)
        fv = jnp.zeros((8, LANES), F32)
        for lag in range(3):
            fk = fk + feature[1, pl.ds(lag, 1), at] * k16[8 - lag : 16 - lag]
            fv = fv + feature[2, pl.ds(lag, 1), at] * v16[8 - lag : 16 - lag]
        packed = jnp.where(
            row8 < 2, pltpu.roll(q16[8:], 2, 0),
            jnp.where(row8 < 4, pltpu.roll(k16[8:], 4, 0), pltpu.roll(v16[8:], 6, 0)),
        )
        edge_out[:, at] = jnp.concatenate([fk * fv, packed], axis=0).astype(BF16)

    def signal_rows(g, count):
        at = cols(g)
        feats = []
        for stream, ref in enumerate((q, k, v)):
            own = ref[pl.ds(0, count), at].astype(F32)
            ext[stream, pl.ds(8, count), :] = own
            total = feature[stream, pl.ds(0, 1), at] * own
            for lag in range(1, 3):
                total = total + feature[stream, pl.ds(lag, 1), at] * ext[stream, pl.ds(8 - lag, count), :]
            feats.append(total)
        gated = feats[1] * feats[2]
        ext[3, pl.ds(8, count), :] = gated
        total = inner[pl.ds(0, 1), at] * gated
        for lag in range(1, 7):
            total = total + inner[pl.ds(lag, 1), at] * ext[3, pl.ds(8 - lag, count), :]
        return key[pl.ds(0, count), at].astype(F32) * (feats[0] * total)

    def low(count):
        return lax.broadcasted_iota(jnp.int32, (count, LANES), 1) < LANES // 2

    def swap(a):
        return pltpu.roll(a, LANES // 2, a.ndim - 1)

    pl.semaphore_wait(barrier, n + 1)

    edge_copy = pltpu.make_async_remote_copy(
        src_ref=edge_out, dst_ref=edge_in, send_sem=edge_sem.at[0], recv_sem=edge_sem.at[1],
        device_id={"ctx": right}, device_id_type=MESH,
    )
    edge_copy.start()

    @pl.loop(1, n)
    def _(s):
        g = other(s)
        pltpu.make_async_remote_copy(
            src_ref=filter_hbm.at[share(part), cols(g)], dst_ref=filt_in.at[me, share(part)],
            send_sem=filt_send, recv_sem=filt_recv.at[me],
            device_id={"ctx": g}, device_id_type=MESH,
        ).start()

    for load in loads[10:]:
        load.start()
    for load in loads[4:9]:
        load.wait()

    def signal_send(half, at, s):
        g = other(s)
        pltpu.make_async_remote_copy(
            src_ref=sig_out.at[half, g, at], dst_ref=sig_in.at[half, me, at],
            send_sem=sig_send, recv_sem=sig_recv.at[half, me],
            device_id={"ctx": g}, device_id_type=MESH,
        ).start()

    ext[:, pl.ds(0, 8), :] = jnp.zeros((4, 8, LANES), F32)

    @pl.loop(1, n + 1)
    def _(s):
        g = other(s)
        block = signal_rows(g, rows)
        upper, lower = block[:mid], swap(block[mid:])
        sig_out[0, g] = jnp.where(low(mid), upper, lower).astype(BF16)
        sig_out[1, g] = jnp.where(low(mid), lower, upper).astype(BF16)

        @pl.when(s < n)
        def _():
            signal_send(0, pl.ds(16, mid - 16), s)

    edge_copy.wait()

    def signal_edge(g):
        edge = jnp.where(me > 0, edge_in[:, cols(g)].astype(F32), 0.0)
        for stream in range(3):
            ext[stream, pl.ds(0, 8), :] = pltpu.roll(edge[8:], 6 - 2 * stream, 0)
        ext[3, pl.ds(0, 8), :] = edge[:8]
        top = signal_rows(g, 16)
        at = pl.ds(0, 16)
        sig_out[0, g, at] = jnp.where(low(16), top, sig_out[0, g, at].astype(F32)).astype(BF16)
        sig_out[1, g, at] = jnp.where(low(16), sig_out[1, g, at].astype(F32), top).astype(BF16)

    @pl.loop(1, n)
    def _(s):
        signal_edge(other(s))
        signal_send(0, pl.ds(0, 16), s)

    signal_edge(me)
    for half in range(2):
        sig_in[half, me] = sig_out[half, me]

    @pl.loop(1, n)
    def _(s):
        g = other(s)
        arrived(filt_in.at[g, share(part)], filt_recv.at[g])

    loads[9].wait()

    def share_copy(at, to, ref):
        return pltpu.make_async_remote_copy(
            src_ref=ref, dst_ref=ref, send_sem=share_send.at[at], recv_sem=share_recv.at[at],
            device_id={"dp": to}, device_id_type=MESH,
        )

    chunks = [pl.ds(c * (n // 4), n // 4) for c in range(4)]
    shares = [share_copy(c, above, filt_in.at[chunks[c], share(part)]) for c in range(4)]
    shares += [share_copy(4 + c, below, filt_in.at[chunks[c], share(part)]) for c in range(4)]
    shares += [share_copy(8 + c, above, filt_in.at[chunks[c], share(below)]) for c in range(2)]
    shares += [share_copy(8 + c, below, filt_in.at[chunks[c], share(above)]) for c in range(2, 4)]
    for at in (0, 6, 1, 7, 2, 4, 3, 5):
        shares[at].start()

    @pl.loop(1, n)
    def _(s):
        signal_send(1, pl.ds(0, mid), s)

    for load in loads[10:]:
        load.wait()

    def first_step(source, j):
        at = [pl.ds(j * 32 + 16 * u if isinstance(j, int) else pl.multiple_of(j * 32 + 16 * u, 16), 16) for u in range(2)]
        pair = jnp.concatenate([source[:, a, :].reshape(n * 16, LANES) for a in at], axis=1)
        done = jnp.dot(first[...], pair, preferred_element_type=F32)
        return [(at[u], done[:, u * LANES : (u + 1) * LANES]) for u in range(2)]

    def filter_step(d):
        for at, done in first_step(filt_in, d):
            filt_spec[:, at, :] = done.astype(BF16).reshape(2 * n, 16, LANES)

    filter_step(part)
    for fore, rear in ((0, 2), (1, 3)):
        arrived(filt_in.at[chunks[fore], share(below)], share_recv.at[fore])
        shares[8 + fore].start()
        arrived(filt_in.at[chunks[rear], share(above)], share_recv.at[4 + rear])
        shares[8 + rear].start()
    for c in (2, 3):
        arrived(filt_in.at[chunks[c], share(below)], share_recv.at[c])
    filter_step(below)
    for c in (0, 1):
        arrived(filt_in.at[chunks[c], share(above)], share_recv.at[4 + c])
    filter_step(above)

    row = lax.broadcasted_iota(jnp.int32, (rows, LANES), 0)

    for half in range(2):
        @pl.loop(1, n)
        def _(s):
            g = other(s)
            arrived(sig_in.at[half, g], sig_recv.at[half, g])

        for j in range(mid // 32):
            for at, done in first_step(sig_in.at[half], j):
                lower = pl.ds(at.start + mid, 16)
                sig_spec[:, at, :] = done.astype(BF16).reshape(2 * n, 16, LANES)
                sig_spec[:, lower, :] = swap(done).astype(BF16).reshape(2 * n, 16, LANES)

        if half == 0:
            for c in range(4):
                arrived(filt_in.at[chunks[c], share(opposite)], share_recv.at[8 + c])
            filter_step(opposite)

        @pl.loop(0, n // UNROLL)
        def _(step):
            for u in range(UNROLL):
                p = step * UNROLL + u
                both = sig_spec[pl.ds(2 * p, 2)].reshape(2 * rows, LANES)
                if half == 0:
                    both = jnp.concatenate([both, filt_spec[pl.ds(2 * p, 2)].reshape(2 * rows, LANES)], axis=1)
                both = jnp.dot(ahead[p], both, preferred_element_type=F32)
                if half == 0:
                    both, freq = both[:, :LANES], both[:, LANES:]
                    filt_freq[p] = freq
                else:
                    freq = filt_freq[p]
                xr, hr, xi, hi = both[:rows], freq[:rows], both[rows:], freq[rows:]
                real, imag = xr * hr - xi * hi, xr * hi + xi * hr
                if u == 0:
                    alone = jnp.logical_and(row == 0, p == 0)
                    real = jnp.where(alone, xr * hr, real)
                    imag = jnp.where(alone, xi * hi, imag)
                product[p, :rows] = real.astype(BF16)
                product[p, rows:] = imag.astype(BF16)

        @pl.loop(0, n // UNROLL)
        def _(step):
            for u in range(UNROLL):
                p = step * UNROLL + u
                both = jnp.dot(back[p], product[p], preferred_element_type=F32).reshape(2, 2, mid, LANES)
                for which in range(2):
                    upper, lower = both[which, 0], swap(both[which, 1])
                    packed = jnp.where(low(mid), upper, lower) if half == 0 else jnp.where(low(mid), lower, upper)
                    turned[2 * p + which] = packed.astype(BF16)

        for j in range(mid // 32):
            at = [pl.ds(j * 32 + 16 * u, 16) for u in range(2)]
            pair = jnp.concatenate([turned[:, a, :].reshape(2 * n * 16, LANES) for a in at], axis=1)
            done = jnp.dot(last[...], pair, preferred_element_type=F32).astype(BF16)
            for u in range(2):
                conv_out[half, :, at[u], :] = done[:, u * LANES : (u + 1) * LANES].reshape(n, 16, LANES)

        @pl.loop(1, n)
        def _(s):
            g = other(s)
            pltpu.make_async_remote_copy(
                src_ref=conv_out.at[half, g], dst_ref=conv_in.at[half, me],
                send_sem=conv_send, recv_sem=conv_recv.at[half, me],
                device_id={"ctx": g}, device_id_type=MESH,
            ).start()

        conv_in[half, me] = conv_out[half, me]

    def finish(g):
        at = cols(g)
        one, two = conv_in[0, g].astype(F32), conv_in[1, g].astype(F32)
        upper = jnp.where(low(mid), one, two)
        lower = swap(jnp.where(low(mid), two, one))
        out[:mid, at] = (query[:mid, at].astype(F32) * upper).astype(BF16)
        out[mid:, at] = (query[mid:, at].astype(F32) * lower).astype(BF16)
        pltpu.make_async_copy(out.at[:, at], out_hbm.at[:, at], out_sem).start()

    finish(me)

    @pl.loop(1, n)
    def _(s):
        g = lax.rem(me + n - s, n)
        for half in range(2):
            arrived(conv_in.at[half, g], conv_recv.at[half, g])
        finish(g)

    arrived(out, out_sem)
    for sent in shares:
        sent.wait_send()
    arrived(filt_in.at[pl.ds(0, n - 1), share(part)], filt_send)
    for ref, sem in ((sig_out, sig_send), (conv_out, conv_send)):
        for half in range(2):
            arrived(ref.at[half, pl.ds(0, n - 1)], sem)


def solution(mesh):
    n, groups = mesh.shape["ctx"], mesh.shape["dp"]

    def local(se_query, se_key, se_value, feature_taps, inner_taps, li_query, li_key, long_filter):
        rows, width = se_query.shape
        tables = transform_tables(n, rows)
        dma = pltpu.SemaphoreType.DMA
        whole = pltpu.VMEM((rows, width), BF16)
        edge = pltpu.VMEM((16, width), BF16)
        halves = pltpu.VMEM((2, n, rows // 2, LANES), BF16)
        spectrum = pltpu.VMEM((2 * n, rows, LANES), BF16)
        return pl.pallas_call(
            functools.partial(kernel, n, groups),
            out_shape=jax.ShapeDtypeStruct((rows, width), BF16),
            in_specs=[pl.BlockSpec(memory_space=pl.ANY)] * 12,
            out_specs=pl.BlockSpec(memory_space=pl.ANY),
            scratch_shapes=[
                whole, whole, whole,
                pltpu.VMEM(feature_taps.shape, F32),
                pltpu.VMEM(inner_taps.shape, F32),
                whole, whole,
                *[pltpu.VMEM(t.shape, BF16) for t in tables],
                pltpu.VMEM((3, 16, width), BF16), edge, edge,
                pltpu.VMEM((4, rows + 8, LANES), F32),
                halves, halves,
                pltpu.VMEM((n, rows, LANES), BF16),
                spectrum, spectrum,
                pltpu.VMEM((n, 2 * rows, LANES), F32),
                pltpu.VMEM((n, 2 * rows, LANES), BF16),
                pltpu.VMEM((2 * n, rows // 2, LANES), BF16),
                halves, halves,
                whole,
                dma((15,)), dma, dma((2,)),
                dma, dma((2, n)),
                dma, dma((n,)),
                dma((12,)), dma((12,)),
                dma, dma((2, n)),
            ],
            compiler_params=pltpu.CompilerParams(
                collective_id=0, has_side_effects=True, vmem_limit_bytes=56 * 1024 * 1024
            ),
        )(
            se_query, se_key, se_value, feature_taps, inner_taps, li_key, li_query, long_filter,
            *[jnp.asarray(t) for t in tables],
        )

    rows_over = P(("dp", "ctx"), None)
    return jax.shard_map(
        local,
        mesh=mesh,
        in_specs=(rows_over, rows_over, rows_over, P(), P(), rows_over, rows_over, P("ctx", None)),
        out_specs=rows_over,
        check_vma=False,
    )
```

```python
import functools

import jax
import jax.numpy as jnp
import ml_dtypes
import numpy as np
from jax import lax
from jax.experimental import pallas as pl
from jax.experimental.pallas import tpu as pltpu
from jax.sharding import PartitionSpec as P

MESH = pl.DeviceIdType.MESH
F32, BF16 = jnp.float32, jnp.bfloat16
LANES = 128
HALF = 16
UNROLL = 16
SIDE = 2
SHARE = 2
SIDES = 4


def transform_tables(blocks, block):
    n = 2 * blocks * block
    i, b, m = np.arange(blocks), np.arange(block), np.arange(block)
    first = np.zeros((blocks, 2, blocks))
    last = np.zeros((blocks, blocks, 2))
    ahead = np.zeros((blocks, 2 * block, 2 * block))
    back = np.zeros((blocks, 2 * block, 2 * block))
    first[0, 0] = 1.0
    first[0, 1] = (-1.0) ** i
    last[:, 0, 0] = 1.0
    last[:, 0, 1] = (-1.0) ** i
    h = block // 2
    even = 2 * np.pi * np.outer(2 * blocks * m[:h], b) / n
    odd = 2 * np.pi * np.outer(blocks + 2 * blocks * m[:h], b) / n
    ahead[0, :h, :block] = np.cos(even)
    ahead[0, block : block + h, :block] = -np.sin(even)
    ahead[0, block, :block] = (-1.0) ** b
    ahead[0, h:block, block:] = np.cos(odd)
    ahead[0, block + h :, block:] = -np.sin(odd)
    back[0, :block, :h] = 2 * np.cos(even).T
    back[0, :block, 0] = 1.0
    back[0, :block, block : block + h] = -2 * np.sin(even).T
    back[0, :block, block] = (-1.0) ** b
    back[0, block:, h:block] = 2 * np.cos(odd).T
    back[0, block:, block + h :] = -2 * np.sin(odd).T
    for p in range(1, blocks):
        turn = np.pi * i * p / blocks
        first[p, 0], first[p, 1] = np.cos(turn), -np.sin(turn)
        last[:, p, 0], last[:, p, 1] = np.cos(turn), -np.sin(turn)
        angle = 2 * np.pi * np.outer(p + 2 * blocks * m, b) / n
        c, s = np.cos(angle), np.sin(angle)
        ahead[p] = np.block([[c, s], [-s, c]])
        back[p] = 2 * np.block([[c.T, -s.T], [s.T, c.T]])
    same = np.eye(HALF)
    first = np.kron(first.reshape(2 * blocks, blocks), same)
    last = np.kron(last.reshape(blocks, 2 * blocks), same)
    return [t.astype(ml_dtypes.bfloat16) for t in (first, ahead, back / n, last)]


def kernel(
    n, groups,
    q_hbm, k_hbm, v_hbm, feature_hbm, inner_hbm, key_hbm, query_hbm, filter_hbm,
    first_hbm, ahead_hbm, back_hbm, last_hbm,
    out_hbm,
    q, k, v, feature, inner, key, query, first, ahead, back, last,
    tails, edge_out, edge_in, ext, filt_rows, filt_out, sig_out, sig_in, filt_in, sig_spec, filt_spec, filt_freq, product, turned,
    conv_out, conv_in, out,
    local_sem, out_sem, edge_sem, sig_send, sig_recv, filt_send, filt_recv, share_send, share_recv,
    conv_send, conv_recv,
):
    me, part = lax.axis_index("ctx"), lax.axis_index("dp")
    right = lax.rem(me + 1, n)
    above, below = lax.rem(part + 1, groups), lax.rem(part + groups - 1, groups)
    opposite = lax.rem(part + 2, groups)
    rows = q.shape[0]
    mid, quarter = rows // 2, rows // groups

    def other(s):
        return lax.rem(me + s, n)

    at_z, at_x, core = me // (2 * SIDES), me // 2 % SIDES, me % 2
    steps = [(0, 0), (0, 1), (1, 0), (0, 3), (3, 0), (1, 1), (3, 3), (1, 3), (3, 1), (0, 2), (2, 0), (1, 2), (2, 1), (3, 2)]
    steps += [(2, 3), (2, 2)]
    on_z = [lax.rem(at_z + d, SIDES) * SIDES for d in range(SIDES)]
    on_x = [lax.rem(at_x + d, SIDES) for d in range(SIDES)]
    chips = [on_z[dz] + on_x[dx] for dz, dx in steps[::-1]]
    peers = [2 * chip + c for chip in chips for c in (1 - core, core)][: n - 1]
    pairs = n // 2

    def cols(g):
        return pl.ds(pl.multiple_of(g * LANES, LANES), LANES)

    def share(d):
        return pl.ds(pl.multiple_of(d * quarter, quarter), quarter)

    def arrived(ref, sem):
        pltpu.make_async_copy(ref, ref, sem).wait()

    tail = pl.ds(rows - 16, 16)
    loads = [
        pltpu.make_async_copy(src, dst, local_sem.at[at])
        for at, (src, dst) in enumerate(
            [
                (q_hbm.at[tail], tails.at[0]), (k_hbm.at[tail], tails.at[1]), (v_hbm.at[tail], tails.at[2]),
                (feature_hbm, feature),
                (filter_hbm.at[share(part)], filt_rows.at[0]), (filter_hbm.at[share(opposite)], filt_rows.at[1]),
                (k_hbm, k), (v_hbm, v), (q_hbm, q), (inner_hbm, inner), (key_hbm, key),
                (first_hbm, first), (ahead_hbm, ahead), (back_hbm, back), (last_hbm, last), (query_hbm, query),
            ]
        )
    ]
    for load in loads[:11]:
        load.start()

    barrier = pltpu.get_barrier_semaphore()

    @pl.loop(1, n)
    def _(s):
        pl.semaphore_signal(barrier, inc=1, device_id={"ctx": other(s)}, device_id_type=MESH)

    for d in (above, below):
        pl.semaphore_signal(barrier, inc=1, device_id={"dp": d}, device_id_type=MESH)

    for load in loads[:4]:
        load.wait()

    def low(count):
        return lax.broadcasted_iota(jnp.int32, (count, LANES), 1) < LANES // 2

    def swap(a):
        return pltpu.roll(a, LANES // 2, a.ndim - 1)

    def spread(upper, lower, half):
        near, far = (upper, lower) if half == 0 else (lower, upper)
        return jnp.where(low(mid), near, swap(far)), jnp.where(low(mid), swap(near), far)

    row8 = lax.broadcasted_iota(jnp.int32, (8, LANES), 0)

    @pl.loop(0, n)
    def _(g):
        at = cols(g)
        q16, k16, v16 = (tails[stream, :, at].astype(F32) for stream in range(3))
        fk = jnp.zeros((8, LANES), F32)
        fv = jnp.zeros((8, LANES), F32)
        for lag in range(3):
            fk = fk + feature[1, pl.ds(lag, 1), at] * k16[8 - lag : 16 - lag]
            fv = fv + feature[2, pl.ds(lag, 1), at] * v16[8 - lag : 16 - lag]
        packed = jnp.where(
            row8 < 2, pltpu.roll(q16[8:], 2, 0),
            jnp.where(row8 < 4, pltpu.roll(k16[8:], 4, 0), pltpu.roll(v16[8:], 6, 0)),
        )
        edge_out[:, at] = jnp.concatenate([fk * fv, packed], axis=0).astype(BF16)

    def signal_rows(g, count, ext):
        at = cols(g)
        feats = []
        for stream, ref in enumerate((q, k, v)):
            own = ref[pl.ds(0, count), at].astype(F32)
            ext[stream, pl.ds(8, count), :] = own
            total = feature[stream, pl.ds(0, 1), at] * own
            for lag in range(1, 3):
                total = total + feature[stream, pl.ds(lag, 1), at] * ext[stream, pl.ds(8 - lag, count), :]
            feats.append(total)
        gated = feats[1] * feats[2]
        ext[3, pl.ds(8, count), :] = gated
        total = inner[pl.ds(0, 1), at] * gated
        for lag in range(1, 7):
            total = total + inner[pl.ds(lag, 1), at] * ext[3, pl.ds(8 - lag, count), :]
        return key[pl.ds(0, count), at].astype(F32) * (feats[0] * total)

    quarters = (part, opposite)
    for which in range(2):
        loads[4 + which].wait()

    @pl.loop(0, pairs)
    def _(j):
        for which in range(2):
            one, two = (filt_rows[which, :, cols(b)].astype(F32) for b in (j, pairs + j))
            filt_out[which, 2 * j] = jnp.where(low(quarter), one, swap(two)).astype(BF16)
            filt_out[which, 2 * j + 1] = jnp.where(low(quarter), swap(one), two).astype(BF16)

    for which in range(2):
        filt_in[me, share(quarters[which]), :] = filt_out[which, me]

    pl.semaphore_wait(barrier, n + 1)

    edge_copy = pltpu.make_async_remote_copy(
        src_ref=edge_out, dst_ref=edge_in, send_sem=edge_sem.at[0], recv_sem=edge_sem.at[1],
        device_id={"ctx": right}, device_id_type=MESH,
    )
    edge_copy.start()

    def filter_copy(which, g):
        return pltpu.make_async_remote_copy(
            src_ref=filt_out.at[which, g], dst_ref=filt_in.at[me, share(quarters[which])],
            send_sem=filt_send.at[which], recv_sem=filt_recv.at[which, me],
            device_id={"ctx": g}, device_id_type=MESH,
        )

    for g in peers:
        filter_copy(0, g).start()

    for load in loads[11:]:
        load.start()
    for load in loads[6:11]:
        load.wait()

    def signal_copy(half, g):
        return pltpu.make_async_remote_copy(
            src_ref=sig_out.at[half, g], dst_ref=sig_in.at[half, me],
            send_sem=sig_send.at[half], recv_sem=sig_recv.at[half, me],
            device_id={"ctx": g}, device_id_type=MESH,
        )

    def signal_pair(half, j, ext):
        block = half * pairs + j
        edge = jnp.where(me > 0, edge_in[:, cols(block)].astype(F32), 0.0)
        for stream in range(3):
            ext[stream, pl.ds(0, 8), :] = pltpu.roll(edge[8:], 6 - 2 * stream, 0)
        ext[3, pl.ds(0, 8), :] = edge[:8]
        rows_of = signal_rows(block, rows, ext)
        for c, packed in enumerate(spread(rows_of[:mid], rows_of[mid:], half)):
            sig_out[half, 2 * j + c] = packed.astype(BF16)

    edge_copy.wait()

    def chip(e):
        place = chips[0]
        for at in range(1, pairs):
            place = jnp.where(e == at, chips[at], place)
        return place

    @pl.loop(0, pairs - SIDE, step=SIDE)
    def _(e):
        places = [chip(e + u) for u in range(SIDE)]
        for u in range(SIDE):
            signal_pair(0, places[u], ext.at[u])
        for j in places:
            for c in range(2):
                signal_copy(0, 2 * j + c).start()

    for u in range(SIDE):
        signal_pair(0, chips[pairs - SIDE + u], ext.at[u])
    for g in peers[2 * (pairs - SIDE) :]:
        signal_copy(0, g).start()
    sig_in[0, me] = sig_out[0, me]

    @pl.loop(1, n)
    def _(s):
        arrived(filt_in.at[other(s), share(part)], filt_recv.at[0, other(s)])

    def share_copy(at, to, piece):
        ref = filt_in.at[pl.ds(piece * SHARE, SHARE), share(part)]
        return pltpu.make_async_remote_copy(
            src_ref=ref, dst_ref=ref, send_sem=share_send.at[at], recv_sem=share_recv.at[at],
            device_id={"dp": to}, device_id_type=MESH,
        )

    for piece in range(n // SHARE):
        for at, to in enumerate((above, below)):
            share_copy(at, to, piece).start()

    for g in peers:
        filter_copy(1, g).start()

    @pl.loop(0, pairs, step=SIDE)
    def _(j):
        for u in range(SIDE):
            signal_pair(1, j + u, ext.at[u])

    sig_in[1, me] = sig_out[1, me]

    for load in loads[11:]:
        load.wait()

    def first_step(source, j):
        at = [pl.ds(j * 32 + 16 * u if isinstance(j, int) else pl.multiple_of(j * 32 + 16 * u, 16), 16) for u in range(2)]
        pair = jnp.concatenate([source[:, a, :].reshape(n * 16, LANES) for a in at], axis=1)
        done = jnp.dot(first[...], pair, preferred_element_type=F32)
        return [(at[u], done[:, u * LANES : (u + 1) * LANES]) for u in range(2)]

    def filter_step(d):
        for at, done in first_step(filt_in, d):
            filt_spec[:, at, :] = done.astype(BF16).reshape(2 * n, 16, LANES)

    filter_step(part)
    arrived(sig_out.at[0, pl.ds(0, n - 1)], sig_send.at[0])
    arrived(filt_out.at[1, pl.ds(0, n - 1)], filt_send.at[1])
    for g in peers:
        signal_copy(1, g).start()

    row = lax.broadcasted_iota(jnp.int32, (rows, LANES), 0)

    for half in range(2):
        @pl.loop(1, n)
        def _(s):
            g = other(s)
            arrived(sig_in.at[half, g], sig_recv.at[half, g])

        for j in range(mid // 32):
            for at, done in first_step(sig_in.at[half], j):
                lower = pl.ds(at.start + mid, 16)
                sig_spec[:, at, :] = done.astype(BF16).reshape(2 * n, 16, LANES)
                sig_spec[:, lower, :] = swap(done).astype(BF16).reshape(2 * n, 16, LANES)

        if half == 0:
            for at, d in enumerate((below, above)):
                arrived(filt_in.at[:, share(d)], share_recv.at[at])
                filter_step(d)

            @pl.loop(1, n)
            def _(s):
                arrived(filt_in.at[other(s), share(opposite)], filt_recv.at[1, other(s)])

            filter_step(opposite)

        @pl.loop(0, n // UNROLL)
        def _(step):
            for u in range(UNROLL):
                p = step * UNROLL + u
                both = sig_spec[pl.ds(2 * p, 2)].reshape(2 * rows, LANES)
                if half == 0:
                    both = jnp.concatenate([both, filt_spec[pl.ds(2 * p, 2)].reshape(2 * rows, LANES)], axis=1)
                both = jnp.dot(ahead[p], both, preferred_element_type=F32)
                if half == 0:
                    both, freq = both[:, :LANES], both[:, LANES:]
                    filt_freq[p] = freq
                else:
                    freq = filt_freq[p]
                xr, hr, xi, hi = both[:rows], freq[:rows], both[rows:], freq[rows:]
                real, imag = xr * hr - xi * hi, xr * hi + xi * hr
                if u == 0:
                    alone = jnp.logical_and(row == 0, p == 0)
                    real = jnp.where(alone, xr * hr, real)
                    imag = jnp.where(alone, xi * hi, imag)
                product[p, :rows] = real.astype(BF16)
                product[p, rows:] = imag.astype(BF16)

        @pl.loop(0, n // UNROLL)
        def _(step):
            for u in range(UNROLL):
                p = step * UNROLL + u
                both = jnp.dot(back[p], product[p], preferred_element_type=F32).reshape(2, 2, mid, LANES)
                for which in range(2):
                    upper, lower = both[which, 0], swap(both[which, 1])
                    packed = jnp.where(low(mid), upper, lower) if half == 0 else jnp.where(low(mid), lower, upper)
                    turned[2 * p + which] = packed.astype(BF16)

        for j in range(mid // 32):
            at = [pl.ds(j * 32 + 16 * u, 16) for u in range(2)]
            pair = jnp.concatenate([turned[:, a, :].reshape(2 * n * 16, LANES) for a in at], axis=1)
            done = jnp.dot(last[...], pair, preferred_element_type=F32).astype(BF16)
            for u in range(2):
                conv_out[half, :, at[u], :] = done[:, u * LANES : (u + 1) * LANES].reshape(n, 16, LANES)

        for g in peers:
            pltpu.make_async_remote_copy(
                src_ref=conv_out.at[half, g], dst_ref=conv_in.at[half, me],
                send_sem=conv_send.at[half], recv_sem=conv_recv.at[half, me],
                device_id={"ctx": g}, device_id_type=MESH,
            ).start()

        conv_in[half, me] = conv_out[half, me]

    def finish(half, j):
        at = cols(half * pairs + j)
        one, two = (conv_in[half, 2 * j + c].astype(F32) for c in range(2))
        upper, lower = jnp.where(low(mid), one, swap(two)), jnp.where(low(mid), swap(one), two)
        if half == 1:
            upper, lower = lower, upper
        out[:mid, at] = (query[:mid, at].astype(F32) * upper).astype(BF16)
        out[mid:, at] = (query[mid:, at].astype(F32) * lower).astype(BF16)
        pltpu.make_async_copy(out.at[:, at], out_hbm.at[:, at], out_sem).start()

    for half in range(2):
        @pl.loop(1, n)
        def _(s):
            arrived(conv_in.at[half, other(s)], conv_recv.at[half, other(s)])

        @pl.loop(0, pairs, step=4)
        def _(j):
            for u in range(4):
                finish(half, j + u)

    arrived(out, out_sem)
    for at in range(2):
        arrived(filt_in.at[:, share(part)], share_send.at[at])

    arrived(sig_out.at[1, pl.ds(0, n - 1)], sig_send.at[1])
    arrived(filt_out.at[0, pl.ds(0, n - 1)], filt_send.at[0])
    for half in range(2):
        arrived(conv_out.at[half, pl.ds(0, n - 1)], conv_send.at[half])


def solution(mesh):
    n, groups = mesh.shape["ctx"], mesh.shape["dp"]

    def local(se_query, se_key, se_value, feature_taps, inner_taps, li_query, li_key, long_filter):
        rows, width = se_query.shape
        tables = transform_tables(n, rows)
        dma = pltpu.SemaphoreType.DMA
        whole = pltpu.VMEM((rows, width), BF16)
        edge = pltpu.VMEM((16, width), BF16)
        halves = pltpu.VMEM((2, n, rows // 2, LANES), BF16)
        spectrum = pltpu.VMEM((2 * n, rows, LANES), BF16)
        return pl.pallas_call(
            functools.partial(kernel, n, groups),
            out_shape=jax.ShapeDtypeStruct((rows, width), BF16),
            in_specs=[pl.BlockSpec(memory_space=pl.ANY)] * 12,
            out_specs=pl.BlockSpec(memory_space=pl.ANY),
            scratch_shapes=[
                whole, whole, whole,
                pltpu.VMEM(feature_taps.shape, F32),
                pltpu.VMEM(inner_taps.shape, F32),
                whole, whole,
                *[pltpu.VMEM(t.shape, BF16) for t in tables],
                pltpu.VMEM((3, 16, width), BF16), edge, edge,
                pltpu.VMEM((SIDE, 4, rows + 8, LANES), F32),
                pltpu.VMEM((2, rows // groups, width), BF16),
                pltpu.VMEM((2, n, rows // groups, LANES), BF16),
                halves, halves,
                pltpu.VMEM((n, rows, LANES), BF16),
                spectrum, spectrum,
                pltpu.VMEM((n, 2 * rows, LANES), F32),
                pltpu.VMEM((n, 2 * rows, LANES), BF16),
                pltpu.VMEM((2 * n, rows // 2, LANES), BF16),
                halves, halves,
                whole,
                dma((16,)), dma, dma((2,)),
                dma((2,)), dma((2, n)),
                dma((2,)), dma((2, n)),
                dma((2,)), dma((2,)),
                dma((2,)), dma((2, n)),
            ],
            compiler_params=pltpu.CompilerParams(
                collective_id=0, has_side_effects=True, vmem_limit_bytes=56 * 1024 * 1024
            ),
        )(
            se_query, se_key, se_value, feature_taps, inner_taps, li_key, li_query, long_filter,
            *[jnp.asarray(t) for t in tables],
        )

    rows_over = P(("dp", "ctx"), None)
    return jax.shard_map(
        local,
        mesh=mesh,
        in_specs=(rows_over, rows_over, rows_over, P(), P(), rows_over, rows_over, P("ctx", None)),
        out_specs=rows_over,
        check_vma=False,
    )
```

```python
import functools

import jax
import jax.numpy as jnp
import ml_dtypes
import numpy as np
from jax import lax
from jax.experimental import pallas as pl
from jax.experimental.pallas import tpu as pltpu
from jax.sharding import PartitionSpec as P

MESH = pl.DeviceIdType.MESH
F32, BF16 = jnp.float32, jnp.bfloat16
LANES = 128
HALF = 16
UNROLL = 32
SIDE = 2
SHARE = 2
SIDES = 4


def transform_tables(blocks, block):
    n = 2 * blocks * block
    i, b, m = np.arange(blocks), np.arange(block), np.arange(block)
    first = np.zeros((blocks, 2, blocks))
    last = np.zeros((blocks, blocks, 2))
    ahead = np.zeros((blocks, 2 * block, 2 * block))
    back = np.zeros((blocks, 2 * block, 2 * block))
    first[0, 0] = 1.0
    first[0, 1] = (-1.0) ** i
    last[:, 0, 0] = 1.0
    last[:, 0, 1] = (-1.0) ** i
    h = block // 2
    even = 2 * np.pi * np.outer(2 * blocks * m[:h], b) / n
    odd = 2 * np.pi * np.outer(blocks + 2 * blocks * m[:h], b) / n
    ahead[0, :h, :block] = np.cos(even)
    ahead[0, block : block + h, :block] = -np.sin(even)
    ahead[0, block, :block] = (-1.0) ** b
    ahead[0, h:block, block:] = np.cos(odd)
    ahead[0, block + h :, block:] = -np.sin(odd)
    back[0, :block, :h] = 2 * np.cos(even).T
    back[0, :block, 0] = 1.0
    back[0, :block, block : block + h] = -2 * np.sin(even).T
    back[0, :block, block] = (-1.0) ** b
    back[0, block:, h:block] = 2 * np.cos(odd).T
    back[0, block:, block + h :] = -2 * np.sin(odd).T
    for p in range(1, blocks):
        turn = np.pi * i * p / blocks
        first[p, 0], first[p, 1] = np.cos(turn), -np.sin(turn)
        last[:, p, 0], last[:, p, 1] = np.cos(turn), -np.sin(turn)
        angle = 2 * np.pi * np.outer(p + 2 * blocks * m, b) / n
        c, s = np.cos(angle), np.sin(angle)
        ahead[p] = np.block([[c, s], [-s, c]])
        back[p] = 2 * np.block([[c.T, -s.T], [s.T, c.T]])
    same = np.eye(HALF)
    first = np.kron(first.reshape(2 * blocks, blocks), same)
    last = np.kron(last.reshape(blocks, 2 * blocks), same)
    return [t.astype(ml_dtypes.bfloat16) for t in (first, ahead, back / n, last)]


def kernel(
    n, groups,
    q_hbm, k_hbm, v_hbm, feature_hbm, inner_hbm, key_hbm, query_hbm, filter_hbm,
    first_hbm, ahead_hbm, back_hbm, last_hbm,
    out,
    q, k, v, feature, inner, key, query, first, ahead, back, last,
    tails, edge_out, edge_in, ext, filt_rows, filt_out, sig_out, sig_in, filt_in, sig_spec, filt_spec, filt_freq, product, turned,
    conv_out, conv_in,
    local_sem, edge_sem, sig_send, sig_recv, filt_send, filt_recv, share_send, share_recv,
    conv_send, conv_recv,
):
    me, part = lax.axis_index("ctx"), lax.axis_index("dp")
    right = lax.rem(me + 1, n)
    above, below = lax.rem(part + 1, groups), lax.rem(part + groups - 1, groups)
    opposite = lax.rem(part + 2, groups)
    rows = q.shape[0]
    mid, quarter = rows // 2, rows // groups

    def other(s):
        return lax.rem(me + s, n)

    at_z, at_x, core = me // (2 * SIDES), me // 2 % SIDES, me % 2
    steps = [(0, 0), (0, 1), (1, 0), (0, 3), (3, 0), (1, 1), (3, 3), (1, 3), (3, 1), (0, 2), (2, 0), (1, 2), (2, 1), (3, 2)]
    steps += [(2, 3), (2, 2)]
    on_z = [lax.rem(at_z + d, SIDES) * SIDES for d in range(SIDES)]
    on_x = [lax.rem(at_x + d, SIDES) for d in range(SIDES)]
    chips = [on_z[dz] + on_x[dx] for dz, dx in steps[::-1]]
    peers = [2 * chip + c for chip in chips for c in (1 - core, core)][: n - 1]
    pairs = n // 2

    def cols(g):
        return pl.ds(pl.multiple_of(g * LANES, LANES), LANES)

    def share(d):
        return pl.ds(pl.multiple_of(d * quarter, quarter), quarter)

    def arrived(ref, sem):
        pltpu.make_async_copy(ref, ref, sem).wait()

    tail = pl.ds(rows - 16, 16)
    loads = [
        pltpu.make_async_copy(src, dst, local_sem.at[at])
        for at, (src, dst) in enumerate(
            [
                (q_hbm.at[tail], tails.at[0]), (k_hbm.at[tail], tails.at[1]), (v_hbm.at[tail], tails.at[2]),
                (feature_hbm, feature),
                (filter_hbm.at[share(part)], filt_rows.at[0]), (filter_hbm.at[share(opposite)], filt_rows.at[1]),
                (k_hbm, k), (v_hbm, v), (q_hbm, q), (inner_hbm, inner), (key_hbm, key),
                (first_hbm, first), (ahead_hbm, ahead), (back_hbm, back), (last_hbm, last), (query_hbm, query),
            ]
        )
    ]
    for load in loads[:11]:
        load.start()

    barrier = pltpu.get_barrier_semaphore()

    @pl.loop(1, n)
    def _(s):
        pl.semaphore_signal(barrier, inc=1, device_id={"ctx": other(s)}, device_id_type=MESH)

    for d in (above, below):
        pl.semaphore_signal(barrier, inc=1, device_id={"dp": d}, device_id_type=MESH)

    for load in loads[:4]:
        load.wait()

    def low(count):
        return lax.broadcasted_iota(jnp.int32, (count, LANES), 1) < LANES // 2

    def swap(a):
        return pltpu.roll(a, LANES // 2, a.ndim - 1)

    def spread(upper, lower, half):
        near, far = (upper, lower) if half == 0 else (lower, upper)
        return jnp.where(low(mid), near, swap(far)), jnp.where(low(mid), swap(near), far)

    row8 = lax.broadcasted_iota(jnp.int32, (8, LANES), 0)

    @pl.loop(0, n)
    def _(g):
        at = cols(g)
        q16, k16, v16 = (tails[stream, :, at].astype(F32) for stream in range(3))
        fk = jnp.zeros((8, LANES), F32)
        fv = jnp.zeros((8, LANES), F32)
        for lag in range(3):
            fk = fk + feature[1, pl.ds(lag, 1), at] * k16[8 - lag : 16 - lag]
            fv = fv + feature[2, pl.ds(lag, 1), at] * v16[8 - lag : 16 - lag]
        packed = jnp.where(
            row8 < 2, pltpu.roll(q16[8:], 2, 0),
            jnp.where(row8 < 4, pltpu.roll(k16[8:], 4, 0), pltpu.roll(v16[8:], 6, 0)),
        )
        edge_out[:, at] = jnp.concatenate([fk * fv, packed], axis=0).astype(BF16)

    def signal_rows(g, count, ext):
        at = cols(g)
        feats = []
        for stream, ref in enumerate((q, k, v)):
            own = ref[pl.ds(0, count), at].astype(F32)
            ext[stream, pl.ds(8, count), :] = own
            total = feature[stream, pl.ds(0, 1), at] * own
            for lag in range(1, 3):
                total = total + feature[stream, pl.ds(lag, 1), at] * ext[stream, pl.ds(8 - lag, count), :]
            feats.append(total)
        gated = feats[1] * feats[2]
        ext[3, pl.ds(8, count), :] = gated
        total = inner[pl.ds(0, 1), at] * gated
        for lag in range(1, 7):
            total = total + inner[pl.ds(lag, 1), at] * ext[3, pl.ds(8 - lag, count), :]
        return key[pl.ds(0, count), at].astype(F32) * (feats[0] * total)

    quarters = (part, opposite)
    for which in range(2):
        loads[4 + which].wait()

    @pl.loop(0, pairs)
    def _(j):
        for which in range(2):
            one, two = (filt_rows[which, :, cols(b)].astype(F32) for b in (j, pairs + j))
            filt_out[which, 2 * j] = jnp.where(low(quarter), one, swap(two)).astype(BF16)
            filt_out[which, 2 * j + 1] = jnp.where(low(quarter), swap(one), two).astype(BF16)

    for which in range(2):
        filt_in[me, share(quarters[which]), :] = filt_out[which, me]

    pl.semaphore_wait(barrier, n + 1)

    edge_copy = pltpu.make_async_remote_copy(
        src_ref=edge_out, dst_ref=edge_in, send_sem=edge_sem.at[0], recv_sem=edge_sem.at[1],
        device_id={"ctx": right}, device_id_type=MESH,
    )
    edge_copy.start()

    def filter_copy(which, g):
        return pltpu.make_async_remote_copy(
            src_ref=filt_out.at[which, g], dst_ref=filt_in.at[me, share(quarters[which])],
            send_sem=filt_send.at[which], recv_sem=filt_recv.at[which, me],
            device_id={"ctx": g}, device_id_type=MESH,
        )

    for g in peers:
        filter_copy(0, g).start()

    for load in loads[11:]:
        load.start()
    for load in loads[6:11]:
        load.wait()

    def signal_copy(half, g):
        return pltpu.make_async_remote_copy(
            src_ref=sig_out.at[half, g], dst_ref=sig_in.at[half, me],
            send_sem=sig_send.at[half], recv_sem=sig_recv.at[half, me],
            device_id={"ctx": g}, device_id_type=MESH,
        )

    def signal_pair(half, j, ext):
        block = half * pairs + j
        edge = jnp.where(me > 0, edge_in[:, cols(block)].astype(F32), 0.0)
        for stream in range(3):
            ext[stream, pl.ds(0, 8), :] = pltpu.roll(edge[8:], 6 - 2 * stream, 0)
        ext[3, pl.ds(0, 8), :] = edge[:8]
        rows_of = signal_rows(block, rows, ext)
        for c, packed in enumerate(spread(rows_of[:mid], rows_of[mid:], half)):
            sig_out[half, 2 * j + c] = packed.astype(BF16)

    edge_copy.wait()

    def chip(e):
        place = chips[0]
        for at in range(1, pairs):
            place = jnp.where(e == at, chips[at], place)
        return place

    @pl.loop(0, pairs - SIDE, step=SIDE)
    def _(e):
        places = [chip(e + u) for u in range(SIDE)]
        for u in range(SIDE):
            signal_pair(0, places[u], ext.at[u])
        for j in places:
            for c in range(2):
                signal_copy(0, 2 * j + c).start()

    for u in range(SIDE):
        signal_pair(0, chips[pairs - SIDE + u], ext.at[u])
    for g in peers[2 * (pairs - SIDE) :]:
        signal_copy(0, g).start()
    sig_in[0, me] = sig_out[0, me]

    @pl.loop(1, n)
    def _(s):
        arrived(filt_in.at[other(s), share(part)], filt_recv.at[0, other(s)])

    def share_copy(at, to, piece):
        ref = filt_in.at[pl.ds(piece * SHARE, SHARE), share(part)]
        return pltpu.make_async_remote_copy(
            src_ref=ref, dst_ref=ref, send_sem=share_send.at[at], recv_sem=share_recv.at[at],
            device_id={"dp": to}, device_id_type=MESH,
        )

    for piece in range(n // SHARE):
        for at, to in enumerate((above, below)):
            share_copy(at, to, piece).start()

    for g in peers:
        filter_copy(1, g).start()

    @pl.loop(0, pairs, step=SIDE)
    def _(j):
        for u in range(SIDE):
            signal_pair(1, j + u, ext.at[u])

    sig_in[1, me] = sig_out[1, me]

    for load in loads[11:]:
        load.wait()

    def first_step(source, j):
        at = [pl.ds(j * 32 + 16 * u if isinstance(j, int) else pl.multiple_of(j * 32 + 16 * u, 16), 16) for u in range(2)]
        pair = jnp.concatenate([source[:, a, :].reshape(n * 16, LANES) for a in at], axis=1)
        done = jnp.dot(first[...], pair, preferred_element_type=F32)
        return [(at[u], done[:, u * LANES : (u + 1) * LANES]) for u in range(2)]

    def filter_step(d):
        for at, done in first_step(filt_in, d):
            filt_spec[:, at, :] = done.astype(BF16).reshape(2 * n, 16, LANES)

    filter_step(part)
    arrived(sig_out.at[0, pl.ds(0, n - 1)], sig_send.at[0])
    arrived(filt_out.at[1, pl.ds(0, n - 1)], filt_send.at[1])
    for g in peers:
        signal_copy(1, g).start()

    row = lax.broadcasted_iota(jnp.int32, (rows, LANES), 0)

    for half in range(2):
        @pl.loop(1, n)
        def _(s):
            g = other(s)
            arrived(sig_in.at[half, g], sig_recv.at[half, g])

        for j in range(mid // 32):
            for at, done in first_step(sig_in.at[half], j):
                lower = pl.ds(at.start + mid, 16)
                sig_spec[:, at, :] = done.astype(BF16).reshape(2 * n, 16, LANES)
                sig_spec[:, lower, :] = swap(done).astype(BF16).reshape(2 * n, 16, LANES)

        if half == 0:
            for at, d in enumerate((below, above)):
                arrived(filt_in.at[:, share(d)], share_recv.at[at])
                filter_step(d)

            @pl.loop(1, n)
            def _(s):
                arrived(filt_in.at[other(s), share(opposite)], filt_recv.at[1, other(s)])

            filter_step(opposite)

        @pl.loop(0, n // UNROLL)
        def _(step):
            for u in range(UNROLL):
                p = step * UNROLL + u
                both = sig_spec[pl.ds(2 * p, 2)].reshape(2 * rows, LANES)
                if half == 0:
                    both = jnp.concatenate([both, filt_spec[pl.ds(2 * p, 2)].reshape(2 * rows, LANES)], axis=1)
                both = jnp.dot(ahead[p], both, preferred_element_type=F32)
                if half == 0:
                    both, freq = both[:, :LANES], both[:, LANES:]
                    filt_freq[p] = freq
                else:
                    freq = filt_freq[p]
                xr, hr, xi, hi = both[:rows], freq[:rows], both[rows:], freq[rows:]
                real, imag = xr * hr - xi * hi, xr * hi + xi * hr
                if u == 0:
                    alone = jnp.logical_and(row == 0, p == 0)
                    real = jnp.where(alone, xr * hr, real)
                    imag = jnp.where(alone, xi * hi, imag)
                product[p, :rows] = real.astype(BF16)
                product[p, rows:] = imag.astype(BF16)

        @pl.loop(0, n // UNROLL)
        def _(step):
            for u in range(UNROLL):
                p = step * UNROLL + u
                both = jnp.dot(back[p], product[p], preferred_element_type=F32).reshape(2, 2, mid, LANES)
                for which in range(2):
                    upper, lower = both[which, 0], swap(both[which, 1])
                    packed = jnp.where(low(mid), upper, lower) if half == 0 else jnp.where(low(mid), lower, upper)
                    turned[2 * p + which] = packed.astype(BF16)

        for j in range(mid // 32):
            at = [pl.ds(j * 32 + 16 * u, 16) for u in range(2)]
            pair = jnp.concatenate([turned[:, a, :].reshape(2 * n * 16, LANES) for a in at], axis=1)
            done = jnp.dot(last[...], pair, preferred_element_type=F32).astype(BF16)
            for u in range(2):
                conv_out[half, :, at[u], :] = done[:, u * LANES : (u + 1) * LANES].reshape(n, 16, LANES)

        for g in peers:
            pltpu.make_async_remote_copy(
                src_ref=conv_out.at[half, g], dst_ref=conv_in.at[half, me],
                send_sem=conv_send.at[half], recv_sem=conv_recv.at[half, me],
                device_id={"ctx": g}, device_id_type=MESH,
            ).start()

        conv_in[half, me] = conv_out[half, me]

    def finish(half, j):
        at = cols(half * pairs + j)
        one, two = (conv_in[half, 2 * j + c].astype(F32) for c in range(2))
        upper, lower = jnp.where(low(mid), one, swap(two)), jnp.where(low(mid), swap(one), two)
        if half == 1:
            upper, lower = lower, upper
        out[:mid, at] = (query[:mid, at].astype(F32) * upper).astype(BF16)
        out[mid:, at] = (query[mid:, at].astype(F32) * lower).astype(BF16)

    for half in range(2):
        for e in range(0, pairs, 4):
            for at in range(2 * e, min(2 * e + 8, n - 1)):
                arrived(conv_in.at[half, peers[at]], conv_recv.at[half, peers[at]])
            for j in chips[e : e + 4]:
                finish(half, j)

    for at in range(2):
        arrived(filt_in.at[:, share(part)], share_send.at[at])

    arrived(sig_out.at[1, pl.ds(0, n - 1)], sig_send.at[1])
    arrived(filt_out.at[0, pl.ds(0, n - 1)], filt_send.at[0])
    for half in range(2):
        arrived(conv_out.at[half, pl.ds(0, n - 1)], conv_send.at[half])


def solution(mesh):
    n, groups = mesh.shape["ctx"], mesh.shape["dp"]

    def local(se_query, se_key, se_value, feature_taps, inner_taps, li_query, li_key, long_filter):
        rows, width = se_query.shape
        tables = transform_tables(n, rows)
        dma = pltpu.SemaphoreType.DMA
        whole = pltpu.VMEM((rows, width), BF16)
        edge = pltpu.VMEM((16, width), BF16)
        halves = pltpu.VMEM((2, n, rows // 2, LANES), BF16)
        spectrum = pltpu.VMEM((2 * n, rows, LANES), BF16)
        return pl.pallas_call(
            functools.partial(kernel, n, groups),
            out_shape=pltpu.VMEM((rows, width), BF16),
            in_specs=[pl.BlockSpec(memory_space=pl.ANY)] * 12,
            out_specs=pl.BlockSpec(memory_space=pltpu.VMEM),
            scratch_shapes=[
                whole, whole, whole,
                pltpu.VMEM(feature_taps.shape, F32),
                pltpu.VMEM(inner_taps.shape, F32),
                whole, whole,
                *[pltpu.VMEM(t.shape, BF16) for t in tables],
                pltpu.VMEM((3, 16, width), BF16), edge, edge,
                pltpu.VMEM((SIDE, 4, rows + 8, LANES), F32),
                pltpu.VMEM((2, rows // groups, width), BF16),
                pltpu.VMEM((2, n, rows // groups, LANES), BF16),
                halves, halves,
                pltpu.VMEM((n, rows, LANES), BF16),
                spectrum, spectrum,
                pltpu.VMEM((n, 2 * rows, LANES), F32),
                pltpu.VMEM((n, 2 * rows, LANES), BF16),
                pltpu.VMEM((2 * n, rows // 2, LANES), BF16),
                halves, halves,
                dma((16,)), dma((2,)),
                dma((2,)), dma((2, n)),
                dma((2,)), dma((2, n)),
                dma((2,)), dma((2,)),
                dma((2,)), dma((2, n)),
            ],
            compiler_params=pltpu.CompilerParams(
                collective_id=0, has_side_effects=True, vmem_limit_bytes=56 * 1024 * 1024
            ),
        )(
            se_query, se_key, se_value, feature_taps, inner_taps, li_key, li_query, long_filter,
            *[jnp.asarray(t) for t in tables],
        )

    rows_over = P(("dp", "ctx"), None)
    return jax.shard_map(
        local,
        mesh=mesh,
        in_specs=(rows_over, rows_over, rows_over, P(), P(), rows_over, rows_over, P("ctx", None)),
        out_specs=rows_over,
        check_vma=False,
    )
```

```python
import functools

import jax
import jax.numpy as jnp
import ml_dtypes
import numpy as np
from jax import lax
from jax.experimental import pallas as pl
from jax.experimental.pallas import tpu as pltpu
from jax.sharding import PartitionSpec as P

MESH = pl.DeviceIdType.MESH
F32, BF16 = jnp.float32, jnp.bfloat16
LANES = 128
HALF = 16
UNROLL = 32
SIDE = 2
SHARE = 2
SIDES = 4


def transform_tables(blocks, block):
    n = 2 * blocks * block
    i, b, m = np.arange(blocks), np.arange(block), np.arange(block)
    first = np.zeros((blocks, 2, blocks))
    last = np.zeros((blocks, blocks, 2))
    ahead = np.zeros((blocks, 2 * block, 2 * block))
    back = np.zeros((blocks, 2 * block, 2 * block))
    first[0, 0] = 1.0
    first[0, 1] = (-1.0) ** i
    last[:, 0, 0] = 1.0
    last[:, 0, 1] = (-1.0) ** i
    h = block // 2
    even = 2 * np.pi * np.outer(2 * blocks * m[:h], b) / n
    odd = 2 * np.pi * np.outer(blocks + 2 * blocks * m[:h], b) / n
    ahead[0, :h, :block] = np.cos(even)
    ahead[0, block : block + h, :block] = -np.sin(even)
    ahead[0, block, :block] = (-1.0) ** b
    ahead[0, h:block, block:] = np.cos(odd)
    ahead[0, block + h :, block:] = -np.sin(odd)
    back[0, :block, :h] = 2 * np.cos(even).T
    back[0, :block, 0] = 1.0
    back[0, :block, block : block + h] = -2 * np.sin(even).T
    back[0, :block, block] = (-1.0) ** b
    back[0, block:, h:block] = 2 * np.cos(odd).T
    back[0, block:, block + h :] = -2 * np.sin(odd).T
    for p in range(1, blocks):
        turn = np.pi * i * p / blocks
        first[p, 0], first[p, 1] = np.cos(turn), -np.sin(turn)
        last[:, p, 0], last[:, p, 1] = np.cos(turn), -np.sin(turn)
        angle = 2 * np.pi * np.outer(p + 2 * blocks * m, b) / n
        c, s = np.cos(angle), np.sin(angle)
        ahead[p] = np.block([[c, s], [-s, c]])
        back[p] = 2 * np.block([[c.T, -s.T], [s.T, c.T]])
    same = np.eye(HALF)
    first = np.kron(first.reshape(2 * blocks, blocks), same)
    last = np.kron(last.reshape(blocks, 2 * blocks), same)
    return [t.astype(ml_dtypes.bfloat16) for t in (first, ahead, back / n, last)]


def kernel(
    n, groups,
    q_hbm, k_hbm, v_hbm, feature_hbm, inner_hbm, key_hbm, query_hbm, filter_hbm,
    first_hbm, ahead_hbm, back_hbm, last_hbm,
    out,
    q, k, v, feature, inner, key, query, first, ahead, back, last,
    tails, edge_out, edge_in, ext, filt_rows, filt_out, sig_out, sig_in, filt_in, sig_spec, filt_spec, filt_freq, product, turned,
    conv_out, conv_in,
    local_sem, edge_sem, sig_send, sig_recv, filt_send, filt_recv, share_send, share_recv,
    conv_send, conv_recv,
):
    me, part = lax.axis_index("ctx"), lax.axis_index("dp")
    right = lax.rem(me + 1, n)
    above, below = lax.rem(part + 1, groups), lax.rem(part + groups - 1, groups)
    opposite = lax.rem(part + 2, groups)
    rows = q.shape[0]
    mid, quarter = rows // 2, rows // groups

    def other(s):
        return lax.rem(me + s, n)

    at_z, at_x, core = me // (2 * SIDES), me // 2 % SIDES, me % 2
    steps = [(0, 0), (0, 1), (1, 0), (0, 3), (3, 0), (1, 1), (3, 3), (1, 3), (3, 1), (0, 2), (2, 0), (1, 2), (2, 1), (3, 2)]
    steps += [(2, 3), (2, 2)]
    on_z = [lax.rem(at_z + d, SIDES) * SIDES for d in range(SIDES)]
    on_x = [lax.rem(at_x + d, SIDES) for d in range(SIDES)]
    chips = [on_z[dz] + on_x[dx] for dz, dx in steps[::-1]]
    peers = [2 * chip + c for chip in chips for c in (1 - core, core)][: n - 1]
    pairs = n // 2

    def cols(g):
        return pl.ds(pl.multiple_of(g * LANES, LANES), LANES)

    def share(d):
        return pl.ds(pl.multiple_of(d * quarter, quarter), quarter)

    def arrived(ref, sem):
        pltpu.make_async_copy(ref, ref, sem).wait()

    tail = pl.ds(rows - 16, 16)
    loads = [
        pltpu.make_async_copy(src, dst, local_sem.at[at])
        for at, (src, dst) in enumerate(
            [
                (q_hbm.at[tail], tails.at[0]), (k_hbm.at[tail], tails.at[1]), (v_hbm.at[tail], tails.at[2]),
                (feature_hbm, feature),
                (filter_hbm.at[share(part)], filt_rows.at[0]), (filter_hbm.at[share(opposite)], filt_rows.at[1]),
                (k_hbm, k), (v_hbm, v), (q_hbm, q), (inner_hbm, inner), (key_hbm, key),
                (first_hbm, first), (ahead_hbm, ahead), (back_hbm, back), (last_hbm, last), (query_hbm, query),
            ]
        )
    ]
    for load in loads[:11]:
        load.start()

    barrier = pltpu.get_barrier_semaphore()

    @pl.loop(1, n)
    def _(s):
        pl.semaphore_signal(barrier, inc=1, device_id={"ctx": other(s)}, device_id_type=MESH)

    for d in (above, below):
        pl.semaphore_signal(barrier, inc=1, device_id={"dp": d}, device_id_type=MESH)

    for load in loads[:4]:
        load.wait()

    def low(count):
        return lax.broadcasted_iota(jnp.int32, (count, LANES), 1) < LANES // 2

    def swap(a):
        return pltpu.roll(a, LANES // 2, a.ndim - 1)

    def spread(upper, lower, half):
        near, far = (upper, lower) if half == 0 else (lower, upper)
        return jnp.where(low(mid), near, swap(far)), jnp.where(low(mid), swap(near), far)

    row8 = lax.broadcasted_iota(jnp.int32, (8, LANES), 0)

    @pl.loop(0, n)
    def _(g):
        at = cols(g)
        q16, k16, v16 = (tails[stream, :, at].astype(F32) for stream in range(3))
        fk = jnp.zeros((8, LANES), F32)
        fv = jnp.zeros((8, LANES), F32)
        for lag in range(3):
            fk = fk + feature[1, pl.ds(lag, 1), at] * k16[8 - lag : 16 - lag]
            fv = fv + feature[2, pl.ds(lag, 1), at] * v16[8 - lag : 16 - lag]
        packed = jnp.where(
            row8 < 2, pltpu.roll(q16[8:], 2, 0),
            jnp.where(row8 < 4, pltpu.roll(k16[8:], 4, 0), pltpu.roll(v16[8:], 6, 0)),
        )
        edge_out[:, at] = jnp.concatenate([fk * fv, packed], axis=0).astype(BF16)

    def signal_rows(g, count, ext):
        at = cols(g)
        feats = []
        for stream, ref in enumerate((q, k, v)):
            own = ref[pl.ds(0, count), at].astype(F32)
            ext[stream, pl.ds(8, count), :] = own
            total = feature[stream, pl.ds(0, 1), at] * own
            for lag in range(1, 3):
                total = total + feature[stream, pl.ds(lag, 1), at] * ext[stream, pl.ds(8 - lag, count), :]
            feats.append(total)
        gated = feats[1] * feats[2]
        ext[3, pl.ds(8, count), :] = gated
        total = inner[pl.ds(0, 1), at] * gated
        for lag in range(1, 7):
            total = total + inner[pl.ds(lag, 1), at] * ext[3, pl.ds(8 - lag, count), :]
        return key[pl.ds(0, count), at].astype(F32) * (feats[0] * total)

    quarters = (part, opposite)
    for which in range(2):
        loads[4 + which].wait()

    @pl.loop(0, pairs)
    def _(j):
        for which in range(2):
            one, two = (filt_rows[which, :, cols(b)].astype(F32) for b in (j, pairs + j))
            filt_out[which, 2 * j] = jnp.where(low(quarter), one, swap(two)).astype(BF16)
            filt_out[which, 2 * j + 1] = jnp.where(low(quarter), swap(one), two).astype(BF16)

    for which in range(2):
        filt_in[me, share(quarters[which]), :] = filt_out[which, me]

    pl.semaphore_wait(barrier, n + 1)

    edge_copy = pltpu.make_async_remote_copy(
        src_ref=edge_out, dst_ref=edge_in, send_sem=edge_sem.at[0], recv_sem=edge_sem.at[1],
        device_id={"ctx": right}, device_id_type=MESH,
    )
    edge_copy.start()

    def filter_copy(which, g):
        return pltpu.make_async_remote_copy(
            src_ref=filt_out.at[which, g], dst_ref=filt_in.at[me, share(quarters[which])],
            send_sem=filt_send.at[which], recv_sem=filt_recv.at[which, me],
            device_id={"ctx": g}, device_id_type=MESH,
        )

    for g in peers:
        filter_copy(0, g).start()

    for load in loads[11:]:
        load.start()
    for load in loads[6:11]:
        load.wait()

    def signal_copy(half, g):
        return pltpu.make_async_remote_copy(
            src_ref=sig_out.at[half, g], dst_ref=sig_in.at[half, me],
            send_sem=sig_send.at[half], recv_sem=sig_recv.at[half, me],
            device_id={"ctx": g}, device_id_type=MESH,
        )

    def signal_edge(block, ext):
        edge = jnp.where(me > 0, edge_in[:, cols(block)].astype(F32), 0.0)
        for stream in range(3):
            ext[stream, pl.ds(0, 8), :] = pltpu.roll(edge[8:], 6 - 2 * stream, 0)
        ext[3, pl.ds(0, 8), :] = edge[:8]

    def signal_top(j, ext):
        signal_edge(j, ext)
        top = signal_rows(j, 16, ext)
        at = pl.ds(0, 16)
        sig_out[0, 2 * j, at] = jnp.where(low(16), top, sig_out[0, 2 * j, at].astype(F32)).astype(BF16)
        sig_out[0, 2 * j + 1, at] = jnp.where(low(16), swap(top), sig_out[0, 2 * j + 1, at].astype(F32)).astype(BF16)

    def signal_pair(half, j, ext):
        block = half * pairs + j
        if half == 1:
            signal_edge(block, ext)
        rows_of = signal_rows(block, rows, ext)
        for c, packed in enumerate(spread(rows_of[:mid], rows_of[mid:], half)):
            sig_out[half, 2 * j + c] = packed.astype(BF16)

    for u in range(SIDE):
        ext[u, :, pl.ds(0, 8), :] = jnp.zeros((4, 8, LANES), F32)

    @pl.loop(0, pairs, step=SIDE)
    def _(j):
        for u in range(SIDE):
            signal_pair(0, j + u, ext.at[u])

    edge_copy.wait()

    def chip(e):
        place = chips[0]
        for at in range(1, pairs):
            place = jnp.where(e == at, chips[at], place)
        return place

    @pl.loop(0, pairs - SIDE, step=SIDE)
    def _(e):
        places = [chip(e + u) for u in range(SIDE)]
        for u in range(SIDE):
            signal_top(places[u], ext.at[u])
        for j in places:
            for c in range(2):
                signal_copy(0, 2 * j + c).start()

    for u in range(SIDE):
        signal_top(chips[pairs - SIDE + u], ext.at[u])
    for g in peers[2 * (pairs - SIDE) :]:
        signal_copy(0, g).start()
    sig_in[0, me] = sig_out[0, me]

    @pl.loop(1, n)
    def _(s):
        arrived(filt_in.at[other(s), share(part)], filt_recv.at[0, other(s)])

    def share_copy(at, to, piece):
        ref = filt_in.at[pl.ds(piece * SHARE, SHARE), share(part)]
        return pltpu.make_async_remote_copy(
            src_ref=ref, dst_ref=ref, send_sem=share_send.at[at], recv_sem=share_recv.at[at],
            device_id={"dp": to}, device_id_type=MESH,
        )

    for piece in range(n // SHARE):
        for at, to in enumerate((above, below)):
            share_copy(at, to, piece).start()

    for g in peers:
        filter_copy(1, g).start()

    @pl.loop(0, pairs, step=SIDE)
    def _(j):
        for u in range(SIDE):
            signal_pair(1, j + u, ext.at[u])

    sig_in[1, me] = sig_out[1, me]

    for load in loads[11:]:
        load.wait()

    def first_step(source, j):
        at = [pl.ds(j * 32 + 16 * u if isinstance(j, int) else pl.multiple_of(j * 32 + 16 * u, 16), 16) for u in range(2)]
        pair = jnp.concatenate([source[:, a, :].reshape(n * 16, LANES) for a in at], axis=1)
        done = jnp.dot(first[...], pair, preferred_element_type=F32)
        return [(at[u], done[:, u * LANES : (u + 1) * LANES]) for u in range(2)]

    def filter_step(d):
        for at, done in first_step(filt_in, d):
            filt_spec[:, at, :] = done.astype(BF16).reshape(2 * n, 16, LANES)

    filter_step(part)
    arrived(sig_out.at[0, pl.ds(0, n - 1)], sig_send.at[0])
    arrived(filt_out.at[1, pl.ds(0, n - 1)], filt_send.at[1])
    for g in peers:
        signal_copy(1, g).start()

    row = lax.broadcasted_iota(jnp.int32, (rows, LANES), 0)

    for half in range(2):
        @pl.loop(1, n)
        def _(s):
            g = other(s)
            arrived(sig_in.at[half, g], sig_recv.at[half, g])

        for j in range(mid // 32):
            for at, done in first_step(sig_in.at[half], j):
                lower = pl.ds(at.start + mid, 16)
                sig_spec[:, at, :] = done.astype(BF16).reshape(2 * n, 16, LANES)
                sig_spec[:, lower, :] = swap(done).astype(BF16).reshape(2 * n, 16, LANES)

        if half == 0:
            for at, d in enumerate((below, above)):
                arrived(filt_in.at[:, share(d)], share_recv.at[at])
                filter_step(d)

            @pl.loop(1, n)
            def _(s):
                arrived(filt_in.at[other(s), share(opposite)], filt_recv.at[1, other(s)])

            filter_step(opposite)

        @pl.loop(0, n // UNROLL)
        def _(step):
            for u in range(UNROLL):
                p = step * UNROLL + u
                both = sig_spec[pl.ds(2 * p, 2)].reshape(2 * rows, LANES)
                if half == 0:
                    both = jnp.concatenate([both, filt_spec[pl.ds(2 * p, 2)].reshape(2 * rows, LANES)], axis=1)
                both = jnp.dot(ahead[p], both, preferred_element_type=F32)
                if half == 0:
                    both, freq = both[:, :LANES], both[:, LANES:]
                    filt_freq[p] = freq
                else:
                    freq = filt_freq[p]
                xr, hr, xi, hi = both[:rows], freq[:rows], both[rows:], freq[rows:]
                real, imag = xr * hr - xi * hi, xr * hi + xi * hr
                if u == 0:
                    alone = jnp.logical_and(row == 0, p == 0)
                    real = jnp.where(alone, xr * hr, real)
                    imag = jnp.where(alone, xi * hi, imag)
                product[p, :rows] = real.astype(BF16)
                product[p, rows:] = imag.astype(BF16)

        @pl.loop(0, n // UNROLL)
        def _(step):
            for u in range(UNROLL):
                p = step * UNROLL + u
                both = jnp.dot(back[p], product[p], preferred_element_type=F32).reshape(2, 2, mid, LANES)
                for which in range(2):
                    upper, lower = both[which, 0], swap(both[which, 1])
                    packed = jnp.where(low(mid), upper, lower) if half == 0 else jnp.where(low(mid), lower, upper)
                    turned[2 * p + which] = packed.astype(BF16)

        for j in range(mid // 32):
            at = [pl.ds(j * 32 + 16 * u, 16) for u in range(2)]
            pair = jnp.concatenate([turned[:, a, :].reshape(2 * n * 16, LANES) for a in at], axis=1)
            done = jnp.dot(last[...], pair, preferred_element_type=F32).astype(BF16)
            for u in range(2):
                conv_out[half, :, at[u], :] = done[:, u * LANES : (u + 1) * LANES].reshape(n, 16, LANES)

        for g in peers:
            pltpu.make_async_remote_copy(
                src_ref=conv_out.at[half, g], dst_ref=conv_in.at[half, me],
                send_sem=conv_send.at[half], recv_sem=conv_recv.at[half, me],
                device_id={"ctx": g}, device_id_type=MESH,
            ).start()

        conv_in[half, me] = conv_out[half, me]

    def finish(half, j):
        at = cols(half * pairs + j)
        one, two = (conv_in[half, 2 * j + c].astype(F32) for c in range(2))
        upper, lower = jnp.where(low(mid), one, swap(two)), jnp.where(low(mid), swap(one), two)
        if half == 1:
            upper, lower = lower, upper
        out[:mid, at] = (query[:mid, at].astype(F32) * upper).astype(BF16)
        out[mid:, at] = (query[mid:, at].astype(F32) * lower).astype(BF16)

    for half in range(2):
        for e in range(0, pairs, 4):
            for at in range(2 * e, min(2 * e + 8, n - 1)):
                arrived(conv_in.at[half, peers[at]], conv_recv.at[half, peers[at]])
            for j in chips[e : e + 4]:
                finish(half, j)

    for at in range(2):
        arrived(filt_in.at[:, share(part)], share_send.at[at])

    arrived(sig_out.at[1, pl.ds(0, n - 1)], sig_send.at[1])
    arrived(filt_out.at[0, pl.ds(0, n - 1)], filt_send.at[0])
    for half in range(2):
        arrived(conv_out.at[half, pl.ds(0, n - 1)], conv_send.at[half])


def solution(mesh):
    n, groups = mesh.shape["ctx"], mesh.shape["dp"]

    def local(se_query, se_key, se_value, feature_taps, inner_taps, li_query, li_key, long_filter):
        rows, width = se_query.shape
        tables = transform_tables(n, rows)
        dma = pltpu.SemaphoreType.DMA
        whole = pltpu.VMEM((rows, width), BF16)
        edge = pltpu.VMEM((16, width), BF16)
        halves = pltpu.VMEM((2, n, rows // 2, LANES), BF16)
        spectrum = pltpu.VMEM((2 * n, rows, LANES), BF16)
        return pl.pallas_call(
            functools.partial(kernel, n, groups),
            out_shape=pltpu.VMEM((rows, width), BF16),
            in_specs=[pl.BlockSpec(memory_space=pl.ANY)] * 12,
            out_specs=pl.BlockSpec(memory_space=pltpu.VMEM),
            scratch_shapes=[
                whole, whole, whole,
                pltpu.VMEM(feature_taps.shape, F32),
                pltpu.VMEM(inner_taps.shape, F32),
                whole, whole,
                *[pltpu.VMEM(t.shape, BF16) for t in tables],
                pltpu.VMEM((3, 16, width), BF16), edge, edge,
                pltpu.VMEM((SIDE, 4, rows + 8, LANES), F32),
                pltpu.VMEM((2, rows // groups, width), BF16),
                pltpu.VMEM((2, n, rows // groups, LANES), BF16),
                halves, halves,
                pltpu.VMEM((n, rows, LANES), BF16),
                spectrum, spectrum,
                pltpu.VMEM((n, 2 * rows, LANES), F32),
                pltpu.VMEM((n, 2 * rows, LANES), BF16),
                pltpu.VMEM((2 * n, rows // 2, LANES), BF16),
                halves, halves,
                dma((16,)), dma((2,)),
                dma((2,)), dma((2, n)),
                dma((2,)), dma((2, n)),
                dma((2,)), dma((2,)),
                dma((2,)), dma((2, n)),
            ],
            compiler_params=pltpu.CompilerParams(
                collective_id=0, has_side_effects=True, vmem_limit_bytes=56 * 1024 * 1024
            ),
        )(
            se_query, se_key, se_value, feature_taps, inner_taps, li_key, li_query, long_filter,
            *[jnp.asarray(t) for t in tables],
        )

    rows_over = P(("dp", "ctx"), None)
    return jax.shard_map(
        local,
        mesh=mesh,
        in_specs=(rows_over, rows_over, rows_over, P(), P(), rows_over, rows_over, P("ctx", None)),
        out_specs=rows_over,
        check_vma=False,
    )
```

```python
import functools

import jax
import jax.numpy as jnp
import ml_dtypes
import numpy as np
from jax import lax
from jax.experimental import pallas as pl
from jax.experimental.pallas import tpu as pltpu
from jax.sharding import PartitionSpec as P

MESH = pl.DeviceIdType.MESH
F32, BF16 = jnp.float32, jnp.bfloat16
LANES = 128
HALF = 16
UNROLL = 32
SIDE = 2
SHARE = 2
SIDES = 4


def transform_tables(blocks, block):
    n = 2 * blocks * block
    i, b, m = np.arange(blocks), np.arange(block), np.arange(block)
    first = np.zeros((blocks, 2, blocks))
    last = np.zeros((blocks, blocks, 2))
    ahead = np.zeros((blocks, 2 * block, 2 * block))
    back = np.zeros((blocks, 2 * block, 2 * block))
    first[0, 0] = 1.0
    first[0, 1] = (-1.0) ** i
    last[:, 0, 0] = 1.0
    last[:, 0, 1] = (-1.0) ** i
    h = block // 2
    even = 2 * np.pi * np.outer(2 * blocks * m[:h], b) / n
    odd = 2 * np.pi * np.outer(blocks + 2 * blocks * m[:h], b) / n
    ahead[0, :h, :block] = np.cos(even)
    ahead[0, block : block + h, :block] = -np.sin(even)
    ahead[0, block, :block] = (-1.0) ** b
    ahead[0, h:block, block:] = np.cos(odd)
    ahead[0, block + h :, block:] = -np.sin(odd)
    back[0, :block, :h] = 2 * np.cos(even).T
    back[0, :block, 0] = 1.0
    back[0, :block, block : block + h] = -2 * np.sin(even).T
    back[0, :block, block] = (-1.0) ** b
    back[0, block:, h:block] = 2 * np.cos(odd).T
    back[0, block:, block + h :] = -2 * np.sin(odd).T
    for p in range(1, blocks):
        turn = np.pi * i * p / blocks
        first[p, 0], first[p, 1] = np.cos(turn), -np.sin(turn)
        last[:, p, 0], last[:, p, 1] = np.cos(turn), -np.sin(turn)
        angle = 2 * np.pi * np.outer(p + 2 * blocks * m, b) / n
        c, s = np.cos(angle), np.sin(angle)
        ahead[p] = np.block([[c, s], [-s, c]])
        back[p] = 2 * np.block([[c.T, -s.T], [s.T, c.T]])
    same = np.eye(HALF)
    first = np.kron(first.reshape(2 * blocks, blocks), same)
    last = np.kron(last.reshape(blocks, 2 * blocks), same)
    return [t.astype(ml_dtypes.bfloat16) for t in (first, ahead, back / n, last)]


def kernel(
    n, groups,
    q_hbm, k_hbm, v_hbm, feature_hbm, inner_hbm, key_hbm, query_hbm, filter_hbm,
    first_hbm, ahead_hbm, back_hbm, last_hbm,
    out,
    q, k, v, feature, inner, key, query, first, ahead, back, last,
    tails, edge_out, edge_in, ext, filt_rows, filt_out, sig_out, sig_in, filt_in, sig_spec, filt_spec, filt_freq, product, turned,
    conv_out, conv_in,
    local_sem, edge_sem, sig_send, sig_recv, filt_send, filt_recv, share_send, share_recv,
    conv_send, conv_recv,
):
    me, part = lax.axis_index("ctx"), lax.axis_index("dp")
    right = lax.rem(me + 1, n)
    above, below = lax.rem(part + 1, groups), lax.rem(part + groups - 1, groups)
    opposite = lax.rem(part + 2, groups)
    rows = q.shape[0]
    mid, quarter = rows // 2, rows // groups

    def other(s):
        return lax.rem(me + s, n)

    at_z, at_x, core = me // (2 * SIDES), me // 2 % SIDES, me % 2
    steps = [(0, 0), (0, 1), (1, 0), (0, 3), (3, 0), (1, 1), (3, 3), (1, 3), (3, 1), (0, 2), (2, 0), (1, 2), (2, 1), (3, 2)]
    steps += [(2, 3), (2, 2)]
    on_z = [lax.rem(at_z + d, SIDES) * SIDES for d in range(SIDES)]
    on_x = [lax.rem(at_x + d, SIDES) for d in range(SIDES)]
    chips = [on_z[dz] + on_x[dx] for dz, dx in steps[::-1]]
    peers = [2 * chip + c for chip in chips for c in (1 - core, core)][: n - 1]
    pairs = n // 2

    def cols(g):
        return pl.ds(pl.multiple_of(g * LANES, LANES), LANES)

    def share(d):
        return pl.ds(pl.multiple_of(d * quarter, quarter), quarter)

    def arrived(ref, sem):
        pltpu.make_async_copy(ref, ref, sem).wait()

    tail = pl.ds(rows - 16, 16)
    loads = [
        pltpu.make_async_copy(src, dst, local_sem.at[at])
        for at, (src, dst) in enumerate(
            [
                (q_hbm.at[tail], tails.at[0]), (k_hbm.at[tail], tails.at[1]), (v_hbm.at[tail], tails.at[2]),
                (feature_hbm, feature),
                (filter_hbm.at[share(part)], filt_rows.at[0]), (filter_hbm.at[share(opposite)], filt_rows.at[1]),
                (k_hbm, k), (v_hbm, v), (q_hbm, q), (inner_hbm, inner), (key_hbm, key),
                (first_hbm, first), (ahead_hbm, ahead), (back_hbm, back), (last_hbm, last), (query_hbm, query),
            ]
        )
    ]
    for load in loads[:6]:
        load.start()

    barrier = pltpu.get_barrier_semaphore()

    @pl.loop(1, n)
    def _(s):
        pl.semaphore_signal(barrier, inc=1, device_id={"ctx": other(s)}, device_id_type=MESH)

    for d in (above, below):
        pl.semaphore_signal(barrier, inc=1, device_id={"dp": d}, device_id_type=MESH)

    for load in loads[6:11]:
        load.start()
    for load in loads[:4]:
        load.wait()

    def low(count):
        return lax.broadcasted_iota(jnp.int32, (count, LANES), 1) < LANES // 2

    def swap(a):
        return pltpu.roll(a, LANES // 2, a.ndim - 1)

    def spread(upper, lower, half):
        near, far = (upper, lower) if half == 0 else (lower, upper)
        return jnp.where(low(mid), near, swap(far)), jnp.where(low(mid), swap(near), far)

    row8 = lax.broadcasted_iota(jnp.int32, (8, LANES), 0)

    def pack_edge(g):
        at = cols(g)
        q16, k16, v16 = (tails[stream, :, at].astype(F32) for stream in range(3))
        fk = jnp.zeros((8, LANES), F32)
        fv = jnp.zeros((8, LANES), F32)
        for lag in range(3):
            fk = fk + feature[1, pl.ds(lag, 1), at] * k16[8 - lag : 16 - lag]
            fv = fv + feature[2, pl.ds(lag, 1), at] * v16[8 - lag : 16 - lag]
        packed = jnp.where(
            row8 < 2, pltpu.roll(q16[8:], 2, 0),
            jnp.where(row8 < 4, pltpu.roll(k16[8:], 4, 0), pltpu.roll(v16[8:], 6, 0)),
        )
        edge_out[:, at] = jnp.concatenate([fk * fv, packed], axis=0).astype(BF16)

    @pl.loop(0, n, step=4)
    def _(g):
        for u in range(4):
            pack_edge(g + u)

    def signal_rows(g, count, ext):
        at = cols(g)
        feats = []
        for stream, ref in enumerate((q, k, v)):
            own = ref[pl.ds(0, count), at].astype(F32)
            ext[stream, pl.ds(8, count), :] = own
            total = feature[stream, pl.ds(0, 1), at] * own
            for lag in range(1, 3):
                total = total + feature[stream, pl.ds(lag, 1), at] * ext[stream, pl.ds(8 - lag, count), :]
            feats.append(total)
        gated = feats[1] * feats[2]
        ext[3, pl.ds(8, count), :] = gated
        total = inner[pl.ds(0, 1), at] * gated
        for lag in range(1, 7):
            total = total + inner[pl.ds(lag, 1), at] * ext[3, pl.ds(8 - lag, count), :]
        return key[pl.ds(0, count), at].astype(F32) * (feats[0] * total)

    quarters = (part, opposite)
    for which in range(2):
        loads[4 + which].wait()

    def regroup(j):
        for which in range(2):
            one, two = (filt_rows[which, :, cols(b)].astype(F32) for b in (j, pairs + j))
            filt_out[which, 2 * j] = jnp.where(low(quarter), one, swap(two)).astype(BF16)
            filt_out[which, 2 * j + 1] = jnp.where(low(quarter), swap(one), two).astype(BF16)

    @pl.loop(0, pairs, step=4)
    def _(j):
        for u in range(4):
            regroup(j + u)

    for which in range(2):
        filt_in[me, share(quarters[which]), :] = filt_out[which, me]

    pl.semaphore_wait(barrier, n + 1)

    edge_copy = pltpu.make_async_remote_copy(
        src_ref=edge_out, dst_ref=edge_in, send_sem=edge_sem.at[0], recv_sem=edge_sem.at[1],
        device_id={"ctx": right}, device_id_type=MESH,
    )
    edge_copy.start()

    def filter_copy(which, g):
        return pltpu.make_async_remote_copy(
            src_ref=filt_out.at[which, g], dst_ref=filt_in.at[me, share(quarters[which])],
            send_sem=filt_send.at[which], recv_sem=filt_recv.at[which, me],
            device_id={"ctx": g}, device_id_type=MESH,
        )

    for g in peers:
        filter_copy(0, g).start()

    for load in loads[11:]:
        load.start()
    for load in loads[6:11]:
        load.wait()

    def signal_copy(half, g):
        return pltpu.make_async_remote_copy(
            src_ref=sig_out.at[half, g], dst_ref=sig_in.at[half, me],
            send_sem=sig_send.at[half], recv_sem=sig_recv.at[half, me],
            device_id={"ctx": g}, device_id_type=MESH,
        )

    def signal_edge(block, ext):
        edge = jnp.where(me > 0, edge_in[:, cols(block)].astype(F32), 0.0)
        for stream in range(3):
            ext[stream, pl.ds(0, 8), :] = pltpu.roll(edge[8:], 6 - 2 * stream, 0)
        ext[3, pl.ds(0, 8), :] = edge[:8]

    def signal_top(j, ext):
        signal_edge(j, ext)
        top = signal_rows(j, 16, ext)
        at = pl.ds(0, 16)
        sig_out[0, 2 * j, at] = jnp.where(low(16), top, sig_out[0, 2 * j, at].astype(F32)).astype(BF16)
        sig_out[0, 2 * j + 1, at] = jnp.where(low(16), swap(top), sig_out[0, 2 * j + 1, at].astype(F32)).astype(BF16)

    def signal_pair(half, j, ext):
        block = half * pairs + j
        if half == 1:
            signal_edge(block, ext)
        rows_of = signal_rows(block, rows, ext)
        for c, packed in enumerate(spread(rows_of[:mid], rows_of[mid:], half)):
            sig_out[half, 2 * j + c] = packed.astype(BF16)

    for u in range(SIDE):
        ext[u, :, pl.ds(0, 8), :] = jnp.zeros((4, 8, LANES), F32)

    @pl.loop(0, pairs, step=SIDE)
    def _(j):
        for u in range(SIDE):
            signal_pair(0, j + u, ext.at[u])

    edge_copy.wait()

    def chip(e):
        place = chips[0]
        for at in range(1, pairs):
            place = jnp.where(e == at, chips[at], place)
        return place

    @pl.loop(0, pairs - SIDE, step=SIDE)
    def _(e):
        places = [chip(e + u) for u in range(SIDE)]
        for u in range(SIDE):
            signal_top(places[u], ext.at[u])
        for j in places:
            for c in range(2):
                signal_copy(0, 2 * j + c).start()

    for u in range(SIDE):
        signal_top(chips[pairs - SIDE + u], ext.at[u])
    for g in peers[2 * (pairs - SIDE) :]:
        signal_copy(0, g).start()
    sig_in[0, me] = sig_out[0, me]

    @pl.loop(1, n)
    def _(s):
        arrived(filt_in.at[other(s), share(part)], filt_recv.at[0, other(s)])

    def share_copy(at, to, piece):
        ref = filt_in.at[pl.ds(piece * SHARE, SHARE), share(part)]
        return pltpu.make_async_remote_copy(
            src_ref=ref, dst_ref=ref, send_sem=share_send.at[at], recv_sem=share_recv.at[at],
            device_id={"dp": to}, device_id_type=MESH,
        )

    for piece in range(n // SHARE):
        for at, to in enumerate((above, below)):
            share_copy(at, to, piece).start()

    for g in peers:
        filter_copy(1, g).start()

    @pl.loop(0, pairs, step=SIDE)
    def _(j):
        for u in range(SIDE):
            signal_pair(1, j + u, ext.at[u])

    sig_in[1, me] = sig_out[1, me]

    for load in loads[11:]:
        load.wait()

    def first_step(source, j):
        at = [pl.ds(j * 32 + 16 * u if isinstance(j, int) else pl.multiple_of(j * 32 + 16 * u, 16), 16) for u in range(2)]
        pair = jnp.concatenate([source[:, a, :].reshape(n * 16, LANES) for a in at], axis=1)
        done = jnp.dot(first[...], pair, preferred_element_type=F32)
        return [(at[u], done[:, u * LANES : (u + 1) * LANES]) for u in range(2)]

    def filter_step(d):
        for at, done in first_step(filt_in, d):
            filt_spec[:, at, :] = done.astype(BF16).reshape(2 * n, 16, LANES)

    filter_step(part)
    arrived(sig_out.at[0, pl.ds(0, n - 1)], sig_send.at[0])
    arrived(filt_out.at[1, pl.ds(0, n - 1)], filt_send.at[1])
    for g in peers:
        signal_copy(1, g).start()

    row = lax.broadcasted_iota(jnp.int32, (rows, LANES), 0)

    for half in range(2):
        @pl.loop(1, n)
        def _(s):
            g = other(s)
            arrived(sig_in.at[half, g], sig_recv.at[half, g])

        for j in range(mid // 32):
            for at, done in first_step(sig_in.at[half], j):
                lower = pl.ds(at.start + mid, 16)
                sig_spec[:, at, :] = done.astype(BF16).reshape(2 * n, 16, LANES)
                sig_spec[:, lower, :] = swap(done).astype(BF16).reshape(2 * n, 16, LANES)

        if half == 0:
            for at, d in enumerate((below, above)):
                arrived(filt_in.at[:, share(d)], share_recv.at[at])
                filter_step(d)

            @pl.loop(1, n)
            def _(s):
                arrived(filt_in.at[other(s), share(opposite)], filt_recv.at[1, other(s)])

            filter_step(opposite)

        @pl.loop(0, n // UNROLL)
        def _(step):
            for u in range(UNROLL):
                p = step * UNROLL + u
                both = sig_spec[pl.ds(2 * p, 2)].reshape(2 * rows, LANES)
                if half == 0:
                    both = jnp.concatenate([both, filt_spec[pl.ds(2 * p, 2)].reshape(2 * rows, LANES)], axis=1)
                both = jnp.dot(ahead[p], both, preferred_element_type=F32)
                if half == 0:
                    both, freq = both[:, :LANES], both[:, LANES:]
                    filt_freq[p] = freq
                else:
                    freq = filt_freq[p]
                xr, hr, xi, hi = both[:rows], freq[:rows], both[rows:], freq[rows:]
                real, imag = xr * hr - xi * hi, xr * hi + xi * hr
                if u == 0:
                    alone = jnp.logical_and(row == 0, p == 0)
                    real = jnp.where(alone, xr * hr, real)
                    imag = jnp.where(alone, xi * hi, imag)
                product[p, :rows] = real.astype(BF16)
                product[p, rows:] = imag.astype(BF16)

        @pl.loop(0, n // UNROLL)
        def _(step):
            for u in range(UNROLL):
                p = step * UNROLL + u
                both = jnp.dot(back[p], product[p], preferred_element_type=F32).reshape(2, 2, mid, LANES)
                for which in range(2):
                    upper, lower = both[which, 0], swap(both[which, 1])
                    packed = jnp.where(low(mid), upper, lower) if half == 0 else jnp.where(low(mid), lower, upper)
                    turned[2 * p + which] = packed.astype(BF16)

        for j in range(mid // 32):
            at = [pl.ds(j * 32 + 16 * u, 16) for u in range(2)]
            pair = jnp.concatenate([turned[:, a, :].reshape(2 * n * 16, LANES) for a in at], axis=1)
            done = jnp.dot(last[...], pair, preferred_element_type=F32).astype(BF16)
            for u in range(2):
                conv_out[half, :, at[u], :] = done[:, u * LANES : (u + 1) * LANES].reshape(n, 16, LANES)

        for g in peers:
            pltpu.make_async_remote_copy(
                src_ref=conv_out.at[half, g], dst_ref=conv_in.at[half, me],
                send_sem=conv_send.at[half], recv_sem=conv_recv.at[half, me],
                device_id={"ctx": g}, device_id_type=MESH,
            ).start()

        conv_in[half, me] = conv_out[half, me]

    def finish(half, j):
        at = cols(half * pairs + j)
        one, two = (conv_in[half, 2 * j + c].astype(F32) for c in range(2))
        upper, lower = jnp.where(low(mid), one, swap(two)), jnp.where(low(mid), swap(one), two)
        if half == 1:
            upper, lower = lower, upper
        out[:mid, at] = (query[:mid, at].astype(F32) * upper).astype(BF16)
        out[mid:, at] = (query[mid:, at].astype(F32) * lower).astype(BF16)

    for half in range(2):
        for e in range(0, pairs, 4):
            for at in range(2 * e, min(2 * e + 8, n - 1)):
                arrived(conv_in.at[half, peers[at]], conv_recv.at[half, peers[at]])
            for j in chips[e : e + 4]:
                finish(half, j)

    for at in range(2):
        arrived(filt_in.at[:, share(part)], share_send.at[at])

    arrived(sig_out.at[1, pl.ds(0, n - 1)], sig_send.at[1])
    arrived(filt_out.at[0, pl.ds(0, n - 1)], filt_send.at[0])
    for half in range(2):
        arrived(conv_out.at[half, pl.ds(0, n - 1)], conv_send.at[half])


def solution(mesh):
    n, groups = mesh.shape["ctx"], mesh.shape["dp"]

    def local(se_query, se_key, se_value, feature_taps, inner_taps, li_query, li_key, long_filter):
        rows, width = se_query.shape
        tables = transform_tables(n, rows)
        dma = pltpu.SemaphoreType.DMA
        whole = pltpu.VMEM((rows, width), BF16)
        edge = pltpu.VMEM((16, width), BF16)
        halves = pltpu.VMEM((2, n, rows // 2, LANES), BF16)
        spectrum = pltpu.VMEM((2 * n, rows, LANES), BF16)
        return pl.pallas_call(
            functools.partial(kernel, n, groups),
            out_shape=pltpu.VMEM((rows, width), BF16),
            in_specs=[pl.BlockSpec(memory_space=pl.ANY)] * 12,
            out_specs=pl.BlockSpec(memory_space=pltpu.VMEM),
            scratch_shapes=[
                whole, whole, whole,
                pltpu.VMEM(feature_taps.shape, F32),
                pltpu.VMEM(inner_taps.shape, F32),
                whole, whole,
                *[pltpu.VMEM(t.shape, BF16) for t in tables],
                pltpu.VMEM((3, 16, width), BF16), edge, edge,
                pltpu.VMEM((SIDE, 4, rows + 8, LANES), F32),
                pltpu.VMEM((2, rows // groups, width), BF16),
                pltpu.VMEM((2, n, rows // groups, LANES), BF16),
                halves, halves,
                pltpu.VMEM((n, rows, LANES), BF16),
                spectrum, spectrum,
                pltpu.VMEM((n, 2 * rows, LANES), F32),
                pltpu.VMEM((n, 2 * rows, LANES), BF16),
                pltpu.VMEM((2 * n, rows // 2, LANES), BF16),
                halves, halves,
                dma((16,)), dma((2,)),
                dma((2,)), dma((2, n)),
                dma((2,)), dma((2, n)),
                dma((2,)), dma((2,)),
                dma((2,)), dma((2, n)),
            ],
            compiler_params=pltpu.CompilerParams(
                collective_id=0, has_side_effects=True, vmem_limit_bytes=56 * 1024 * 1024
            ),
        )(
            se_query, se_key, se_value, feature_taps, inner_taps, li_key, li_query, long_filter,
            *[jnp.asarray(t) for t in tables],
        )

    rows_over = P(("dp", "ctx"), None)
    return jax.shard_map(
        local,
        mesh=mesh,
        in_specs=(rows_over, rows_over, rows_over, P(), P(), rows_over, rows_over, P("ctx", None)),
        out_specs=rows_over,
        check_vma=False,
    )
```
